32 devices in a mesh: groups: 2 (over x), tm: 16 (over z, y, core).
Axes of the slice: x: 2, y: 2, z: 4, core: 2. Of those that a mesh axis runs over, the one named last changes fastest.
Arguments:
- inputs: bfloat16 [4096, 1280], P(('groups', 'tm')), parts along dimension 0, may hold values from -12 to 12
- ln_gain: float32 [1280], replicated, may hold values from 0.1 to 1.9
- ln_bias: float32 [1280], replicated, may hold values from -3 to 3
- qkv_weight: bfloat16 [1280, 1920], P('tm'), may hold values from -1 to 1
- v_bias: float32 [640], replicated, may hold values from -3 to 3
- out_weight: bfloat16 [640, 1280], P(None, 'tm'), may hold values from -0.25 to 0.25
- out_bias: float32 [1280], replicated, may hold values from -3 to 3
Outputs:
- updated: bfloat16 [4096, 1280], P(('groups', 'tm')), parts along dimension 0
The draws below stay inside these ranges and needn't reach their ends.
There are 2 independent parts, one for each index of `groups`. The reference program is written for one: setup_inputs(seed, part) draws one part's arguments, and reference() takes and returns one part's arrays. A program takes and returns all parts, laid end to end along the dimension named above; an argument that names none is the same for every part. Nothing has to cross between parts.
All inputs are finite; a program needn't handle non-finite values.
Results may differ from the reference program's by a relative error of at most 0.0065.
Values may be sent and summed in bfloat16 or wider, within the bound.
A program may use at most 192 MiB of HBM per device.

```python
import math
import jax
import jax.numpy as jnp
from jax import lax

D = 1280
HEADS = 10
HEAD_SIZE = 64
TOKENS = 2048


def draw_inputs(key, part):
    key_base = jax.random.fold_in(key, 0)
    drawn = jnp.clip(jax.random.normal(key_base, (TOKENS, D), jnp.float32), -6.0, 6.0)
    return drawn.astype(jnp.bfloat16)


def draw_qkv_weight(key, part):
    head_width = HEADS * HEAD_SIZE
    deviation = jnp.concatenate([jnp.full((2 * head_width,), 1.6, jnp.float32), jnp.ones((head_width,), jnp.float32)]) / math.sqrt(D)
    drawn = jnp.clip(jax.random.normal(key, (D, 3 * head_width), jnp.float32), -4.5, 4.5) * deviation
    return jnp.clip(drawn, -1.0, 1.0).astype(jnp.bfloat16)


def block_scale(stream_key, shape, shards, least, high):
    gain = 1.0
    for axis_at, parts in shards:
        steps = jax.random.uniform(jax.random.fold_in(jax.random.fold_in(stream_key, 6), axis_at), (parts,), jnp.float32, least / len(shards), high / len(shards))
        gain = gain * jnp.repeat(jnp.exp(steps), shape[axis_at] // parts).reshape((-1,) + (1,) * (len(shape) - 1 - axis_at))
    return gain


def bell_draw(stream_key, extent, spread, bound, pieces=(), held_as=jnp.bfloat16):
    loudness = block_scale(stream_key, extent, pieces, -0.22, 0.18) if pieces else 1.0
    array = jax.random.normal(stream_key, extent, jnp.float32) * spread * loudness
    return jnp.minimum(jnp.maximum(array, -bound), bound).astype(held_as)


def setup_inputs(seed: int = 0, part: int = 0) -> dict:
    key_list = jax.random.split(jax.random.key(seed), 8)
    part_keys = jax.random.split(jax.random.fold_in(key_list[7], part), 8)
    return {
        "inputs": draw_inputs(jax.random.fold_in(jax.random.fold_in(key_list[7], part), 71), part),
        "ln_gain": jnp.clip(1.0 + 0.18 * jax.random.normal(key_list[1], (D,), jnp.float32), 0.1, 1.9),
        "ln_bias": bell_draw(key_list[2], (D,), 0.5, 3.0, (), jnp.float32),
        "qkv_weight": draw_qkv_weight(jax.random.fold_in(key_list[7], 71), part),
        "v_bias": bell_draw(key_list[4], (HEADS * HEAD_SIZE,), 0.5, 3.0, (), jnp.float32),
        "out_weight": bell_draw(key_list[5], (HEADS * HEAD_SIZE, D), (HEADS * HEAD_SIZE) ** -0.5, 0.25, ((1, 16),)),
        "out_bias": bell_draw(key_list[6], (D,), 0.5, 3.0, (), jnp.float32),
    }


def layer_norm(inputs, ln_gain, ln_bias):
    widened = inputs.astype(jnp.float32)
    average = lax.optimization_barrier(jnp.mean(widened, -1, keepdims=True))
    centred = widened - average
    variance = lax.optimization_barrier(jnp.mean(centred * centred, -1, keepdims=True))
    return (centred * lax.rsqrt(variance + 1e-05) * ln_gain + ln_bias).astype(jnp.bfloat16)

def reference(inputs, ln_gain, ln_bias, qkv_weight, v_bias, out_weight, out_bias):
    normed = layer_norm(inputs, ln_gain, ln_bias)
    projected = jnp.dot(normed, qkv_weight, preferred_element_type=jnp.float32)
    head_width = HEADS * HEAD_SIZE
    queries = (projected[:, :head_width] * HEAD_SIZE ** (-0.5)).astype(jnp.bfloat16)
    key_rows = projected[:, head_width:2 * head_width].astype(jnp.bfloat16)
    values = (projected[:, 2 * head_width:] + v_bias).astype(jnp.bfloat16)
    block_rows = math.gcd(TOKENS, 512)
    query_blocks = queries.reshape(TOKENS // block_rows, block_rows, HEADS, HEAD_SIZE)
    key_float = key_rows.astype(jnp.float32).reshape(TOKENS, HEADS, HEAD_SIZE)
    value_float = values.astype(jnp.float32).reshape(TOKENS, HEADS, HEAD_SIZE)

    def attend_block(query_block):
        scores = jnp.einsum('qhd,khd->hqk', query_block.astype(jnp.float32), key_float)
        row_max = lax.optimization_barrier(jnp.max(scores, -1, keepdims=True))
        exponent = jnp.exp(scores - row_max)
        row_sum = lax.optimization_barrier(jnp.sum(exponent, -1))
        weights_bf = lax.optimization_barrier(exponent.astype(jnp.bfloat16))
        mixed = jnp.einsum('hqk,khd->hqd', weights_bf.astype(jnp.float32), value_float)
        context = mixed / row_sum[..., None]
        return jnp.transpose(context, (1, 0, 2)).reshape(block_rows, head_width).astype(jnp.bfloat16)
    context = lax.map(attend_block, query_blocks).reshape(TOKENS, head_width)
    projection = jnp.dot(context, out_weight, preferred_element_type=jnp.float32)
    return (inputs.astype(jnp.float32) + projection + out_bias).astype(jnp.bfloat16)
```

```python
import functools

import jax
import jax.numpy as jnp
from jax import lax
from jax.experimental import pallas as pl
from jax.experimental.pallas import tpu as pltpu
from jax.sharding import PartitionSpec as P

HEAD_SIZE = 64


def swapped(value, axis, apart):
    mask = 2**apart
    pairs = [(source, source ^ mask) for source in range(lax.axis_size(axis))]
    return lax.ppermute(value, axis, pairs)


def from_behind(block, axis, distance):
    devices = range(lax.axis_size(axis))
    route = [((i - distance) % len(devices), i) for i in devices]
    return lax.ppermute(block, axis, route)


def layer_norm(inputs, ln_gain, ln_bias):
    widened = inputs.astype(jnp.float32)
    average = jnp.mean(widened, -1, keepdims=True)
    centred = widened - average
    variance = jnp.mean(centred * centred, -1, keepdims=True)
    return (centred * lax.rsqrt(variance + 1e-05) * ln_gain + ln_bias).astype(jnp.bfloat16)


def attend(state_now, queries, key_part, value_part):
    running_max, running_sum, weighted = state_now
    key_count = key_part.shape[0]
    head_count = queries.shape[1]
    key_heads = key_part.reshape(key_count, head_count, HEAD_SIZE)
    value_heads = value_part.reshape(key_count, head_count, HEAD_SIZE)
    scores = jnp.einsum("qhd,khd->hqk", queries, key_heads, preferred_element_type=jnp.float32)
    new_max = jnp.maximum(running_max, jnp.max(scores, -1))
    rescale = jnp.exp(running_max - new_max)
    exponent = jnp.exp(scores - new_max[..., None])
    running_sum = running_sum * rescale + jnp.sum(exponent, -1)
    weights_bf = exponent.astype(jnp.bfloat16)
    weighted = weighted * rescale[..., None] + jnp.einsum(
        "hqk,khd->hqd", weights_bf, value_heads, preferred_element_type=jnp.float32
    )
    return (new_max, running_sum, weighted)


def empty_state(head_count, row_count):
    return (
        jnp.full((head_count, row_count), -jnp.inf, jnp.float32),
        jnp.zeros((head_count, row_count), jnp.float32),
        jnp.zeros((head_count, row_count, HEAD_SIZE), jnp.float32),
    )


def finish(final_state):
    mixed = final_state[2] / final_state[1][..., None]
    head_count, row_count = (mixed.shape[0], mixed.shape[1])
    return (
        jnp.transpose(mixed, (1, 0, 2))
        .reshape(row_count, head_count * HEAD_SIZE)
        .astype(jnp.bfloat16)
    )


def per_device_plain(inputs, ln_gain, ln_bias, qkv_weight, v_bias, out_weight, out_bias):
    normed = layer_norm(inputs, ln_gain, ln_bias)
    row_count = inputs.shape[0]
    head_width = v_bias.shape[0]
    head_count = head_width // HEAD_SIZE
    projected = jnp.dot(
        normed,
        lax.all_gather(qkv_weight, "tm", axis=0, tiled=True),
        preferred_element_type=jnp.float32,
    )
    queries = (projected[:, :head_width] * HEAD_SIZE ** (-0.5)).astype(jnp.bfloat16)
    key_rows = projected[:, head_width : 2 * head_width].astype(jnp.bfloat16)
    values = (projected[:, 2 * head_width :] + v_bias).astype(jnp.bfloat16)
    parity = lax.axis_index("tm") % 2
    half_count = head_count // 2
    half_width = half_count * HEAD_SIZE
    stacked = jnp.stack([queries, key_rows, values])
    keep_part = lax.dynamic_slice_in_dim(stacked, parity * half_width, half_width, 2)
    give_part = lax.dynamic_slice_in_dim(stacked, (1 - parity) * half_width, half_width, 2)
    got_part = swapped(give_part, "tm", 0)
    first_rows = jnp.where(parity == 0, keep_part, got_part)
    second_rows = jnp.where(parity == 0, got_part, keep_part)
    joined = jnp.concatenate([first_rows, second_rows], 1)
    pair_rows = 2 * row_count
    pair_queries = joined[0].reshape(pair_rows, half_count, HEAD_SIZE)
    key_value_block = joined[1:]
    state_now = attend(
        empty_state(half_count, pair_rows), pair_queries, key_value_block[0], key_value_block[1]
    )

    def cycle_turn(step, carry):
        state_now, block_now = carry
        block_now = from_behind(block_now, "tm", 2)
        return (attend(state_now, pair_queries, block_now[0], block_now[1]), block_now)

    final_state, unused_block = lax.fori_loop(
        0, lax.axis_size("tm") // 2 - 1, cycle_turn, (state_now, key_value_block)
    )
    pair_context = finish(final_state)
    mine_rows = lax.dynamic_slice_in_dim(pair_context, parity * row_count, row_count, 0)
    other_rows = lax.dynamic_slice_in_dim(pair_context, (1 - parity) * row_count, row_count, 0)
    back_rows = swapped(other_rows, "tm", 0)
    context = jnp.where(
        parity == 0,
        jnp.concatenate([mine_rows, back_rows], 1),
        jnp.concatenate([back_rows, mine_rows], 1),
    )
    projection = jnp.dot(
        context,
        lax.all_gather(out_weight, "tm", axis=1, tiled=True),
        preferred_element_type=jnp.float32,
    )
    return (inputs.astype(jnp.float32) + projection + out_bias).astype(jnp.bfloat16)


def fused_kernel(
    n,
    x_ref, gain_ref, bias_ref, w_ref, vb_ref, wo_ref, ob_ref,
    o_ref,
    xother, normed, wfull, wpass, kv, qh, top, total, acc, wofull, ctx, ctxfull,
    x_sem, w_send, w_core, w_recv, p_send, p_recv, kv_send, kv_recv, o_send, o_core, o_recv, c_sem,
):
    me = lax.axis_index("tm")
    lines = n // 4
    c = lax.rem(me, 2)
    y = lax.rem(lax.div(me, 2), 2)
    z = lax.div(me, 4)
    rows = x_ref.shape[0]
    wrows = w_ref.shape[0]
    width = wo_ref.shape[0]
    half = width // 2
    heads = half // HEAD_SIZE
    right, left = me + 4, me - 4
    has_right, has_left = z < lines - 1, z > 0
    other_y = me + 2 - 4 * y
    other_c = me + 1 - 2 * c

    def send(src, dst, ssem, rsem, device):
        return pltpu.make_async_remote_copy(
            src_ref=src, dst_ref=dst, send_sem=ssem, recv_sem=rsem,
            device_id={"tm": device}, device_id_type=pl.DeviceIdType.MESH,
        )

    def nth(t):
        near = jnp.minimum(z, lines - 1 - z)
        k = lax.div(t + 1, 2)
        both = jnp.where(lax.rem(t, 2) == 1, z - k, z + k)
        far = t - near
        one = jnp.where(z < lines - 1 - z, z + far, z - far)
        return jnp.where(t <= 2 * near, both, one)

    def w_block(zz, yy, cc):
        return zz * 4 + yy * 2 + cc

    def w_rows(ref, block):
        return ref.at[pl.ds(pl.multiple_of(block * wrows, wrows), wrows), :]

    def w_z(zz, way, device):
        b = w_block(zz, y, c)
        return send(w_rows(wfull, b), w_rows(wfull, b), w_send.at[way, zz], w_recv.at[b], device)

    def p_z(zz, way, device):
        return send(wpass.at[zz], wpass.at[zz], p_send.at[way, zz], p_recv.at[zz], device)

    def p_y(zz):
        b = w_block(zz, y, c)
        return send(wpass.at[zz], w_rows(wfull, b), p_send.at[2, zz], w_recv.at[b], other_y)

    def w_c(zz, yy, cc):
        b = w_block(zz, yy, cc)
        return send(w_rows(wfull, b), w_rows(wfull, b), w_core.at[b], w_recv.at[b], other_c)

    def o_z(zz, way, device):
        b = w_block(zz, y, c)
        return send(w_rows(wofull, b), w_rows(wofull, b), o_send.at[way, zz], o_recv.at[b], device)

    def o_y(zz, yy):
        b = w_block(zz, yy, c)
        return send(w_rows(wofull, b), w_rows(wofull, b), o_send.at[2, zz], o_recv.at[b], other_y)

    def o_c(zz, yy, cc):
        b = w_block(zz, yy, cc)
        return send(w_rows(wofull, b), w_rows(wofull, b), o_core.at[b], o_recv.at[b], other_c)

    def kv_z(zz, way, device):
        b = zz * 2 + c
        return send(kv.at[b], kv.at[b], kv_send.at[way, zz], kv_recv.at[b], device)

    def kv_c(zz, cc):
        b = zz * 2 + cc
        return send(kv.at[b], kv.at[b], kv_send.at[2, zz], kv_recv.at[b], other_c)

    def along(zz, makers):
        @pl.when(jnp.logical_and(zz <= z, has_right))
        def _():
            for maker in makers:
                maker(zz, 0, right).start()

        @pl.when(jnp.logical_and(zz >= z, has_left))
        def _():
            for maker in makers:
                maker(zz, 1, left).start()

    def along_done(zz, makers):
        @pl.when(jnp.logical_and(zz <= z, has_right))
        def _():
            for maker in makers:
                maker(zz, 0, right).wait_send()

        @pl.when(jnp.logical_and(zz >= z, has_left))
        def _():
            for maker in makers:
                maker(zz, 1, left).wait_send()

    barrier = pltpu.get_barrier_semaphore()

    def greet(device):
        pl.semaphore_signal(barrier, inc=1, device_id={"tm": device}, device_id_type=pl.DeviceIdType.MESH)

    greet(other_y)
    greet(other_c)

    @pl.when(has_right)
    def _():
        greet(right)

    @pl.when(has_left)
    def _():
        greet(left)

    mine = pl.ds(pl.multiple_of(me * wrows, wrows), wrows)
    for yy in range(2):

        @pl.when(y == yy)
        def _():
            for at, part in enumerate((1, 2, 0)):
                wide = pl.ds(at * half, half)
                wfull[mine, wide] = w_ref[:, pl.ds(part * width + yy * half, half)]
                wpass[z, :, wide] = w_ref[:, pl.ds(part * width + (1 - yy) * half, half)]

    peers = 2 + jnp.where(has_right, 1, 0) + jnp.where(has_left, 1, 0)
    pl.semaphore_wait(barrier, peers)

    along(z, (p_z, w_z))
    p_y(z).start()
    x_copy = send(x_ref, xother, x_sem.at[0], x_sem.at[1], other_y)
    x_copy.start()
    w_c(z, y, c).start()

    row = lax.broadcasted_iota(jnp.int32, (wrows, wrows), 0)
    column = lax.broadcasted_iota(jnp.int32, (wrows, wrows), 1)
    unit = jnp.where(row == column, 1.0, 0.0).astype(jnp.bfloat16)
    wofull[mine, :] = lax.dot_general(
        unit, wo_ref[...], (((1,), (1,)), ((), ())), preferred_element_type=jnp.float32
    ).astype(jnp.bfloat16)

    def norm_rows(ref, yy):
        widened = ref[...].astype(jnp.float32)
        average = jnp.mean(widened, -1, keepdims=True)
        centred = widened - average
        variance = jnp.mean(centred * centred, -1, keepdims=True)
        normed[pl.ds(pl.multiple_of(yy * rows, rows), rows), :] = (
            centred * lax.rsqrt(variance + 1e-05) * gain_ref[...] + bias_ref[...]
        ).astype(jnp.bfloat16)

    norm_rows(x_ref, y)

    def w_turn(t, carry):
        @pl.when(t < lines)
        def _():
            zz = nth(t)
            p_z(zz, 0, right).wait_recv()
            along(zz, (p_z,))
            p_y(zz).start()
            w_z(zz, 0, right).wait_recv()
            along(zz, (w_z,))
            w_c(zz, y, c).start()

        before = nth(t - 1)
        w_c(before, 1 - y, c).wait_recv()
        w_c(before, 1 - y, c).start()
        return carry

    lax.fori_loop(1, lines + 1, w_turn, 0)

    along(z, (o_z,))
    o_y(z, y).start()
    o_c(z, y, c).start()
    x_copy.wait()
    norm_rows(xother, 1 - y)

    def w_arrived(zz, carry):
        for yy in range(2):
            w_c(zz, yy, 1 - c).wait_recv()
        return carry

    lax.fori_loop(0, lines, w_arrived, 0)

    own = z * 2 + c
    both = normed[...]
    kv[own] = (
        jnp.dot(both, wfull[:, : 2 * half], preferred_element_type=jnp.float32) + vb_ref[y]
    ).astype(jnp.bfloat16)
    along(z, (kv_z,))
    kv_c(z, c).start()
    queries = (
        jnp.dot(both, wfull[:, 2 * half :], preferred_element_type=jnp.float32) * HEAD_SIZE ** (-0.5)
    ).astype(jnp.bfloat16)
    for h in range(heads):
        qh[h] = queries[:, h * HEAD_SIZE : (h + 1) * HEAD_SIZE]
    top[...] = jnp.full_like(top, -jnp.inf)
    total[...] = jnp.zeros_like(total)
    acc[...] = jnp.zeros_like(acc)

    def attend_block(b):
        for h in range(heads):
            key_part = kv[b, :, h * HEAD_SIZE : (h + 1) * HEAD_SIZE]
            value_part = kv[b, :, half + h * HEAD_SIZE : half + (h + 1) * HEAD_SIZE]
            scores = lax.dot_general(
                qh[h], key_part, (((1,), (1,)), ((), ())), preferred_element_type=jnp.float32
            )
            old_top = top[h]
            new_top = jnp.maximum(old_top, jnp.max(scores, -1, keepdims=True))
            rescale = jnp.exp(old_top - new_top)
            exponent = jnp.exp(scores - new_top[:, :1])
            total[h] = total[h] * rescale + jnp.sum(exponent, -1, keepdims=True)
            top[h] = new_top
            acc[h] = acc[h] * rescale[:, :HEAD_SIZE] + jnp.dot(
                exponent.astype(jnp.bfloat16), value_part, preferred_element_type=jnp.float32
            )

    def kv_turn(t, carry):
        zz = nth(t)

        @pl.when(t > 0)
        def _():
            kv_z(zz, 0, right).wait_recv()
            along(zz, (kv_z,))
            kv_c(zz, c).start()
            o_z(zz, 0, right).wait_recv()
            along(zz, (o_z,))
            o_y(zz, y).start()
            o_c(zz, y, c).start()
            before = nth(t - 1)
            o_y(before, 1 - y).wait_recv()
            o_c(before, 1 - y, c).start()

        attend_block(zz * 2 + c)
        kv_c(zz, 1 - c).wait_recv()
        attend_block(zz * 2 + 1 - c)
        return carry

    lax.fori_loop(0, lines, kv_turn, 0)
    last = nth(lines - 1)
    o_y(last, 1 - y).wait_recv()
    o_c(last, 1 - y, c).start()

    for h in range(heads):
        ctx[y, :, h * HEAD_SIZE : (h + 1) * HEAD_SIZE] = (
            acc[h] / total[h][:, :HEAD_SIZE]
        ).astype(jnp.bfloat16)
    theirs = pl.ds(pl.multiple_of((1 - y) * rows, rows), rows)
    ours = pl.ds(pl.multiple_of(y * rows, rows), rows)
    c_copy = send(ctx.at[y, theirs, :], ctx.at[y, theirs, :], c_sem.at[0], c_sem.at[1], other_y)
    c_back = send(ctx.at[1 - y, ours, :], ctx.at[1 - y, ours, :], c_sem.at[0], c_sem.at[1], other_y)
    c_copy.start()

    def drained(zz, carry):
        along_done(zz, (p_z, w_z, kv_z, o_z))
        p_y(zz).wait_send()
        kv_c(zz, c).wait_send()
        o_y(zz, y).wait_send()
        for yy in range(2):
            w_c(zz, yy, c).wait_send()
            o_c(zz, yy, c).wait_send()
            o_c(zz, yy, 1 - c).wait_recv()
        return carry

    lax.fori_loop(0, lines, drained, 0)
    c_copy.wait_send()
    c_back.wait_recv()
    for part in range(2):
        ctxfull[:, part * half : (part + 1) * half] = ctx[part, ours, :]
    projection = lax.dot_general(
        ctxfull[...], wofull[...], (((1,), (1,)), ((), ())), preferred_element_type=jnp.float32
    )
    o_ref[...] = (x_ref[...].astype(jnp.float32) + projection + ob_ref[...]).astype(o_ref.dtype)


def per_device_fused(n, inputs, ln_gain, ln_bias, qkv_weight, v_bias, out_weight, out_bias):
    rows, depth = inputs.shape
    width = v_bias.shape[0]
    half = width // 2
    heads = half // HEAD_SIZE
    lines = n // 4
    wrows = qkv_weight.shape[0]
    halves = v_bias.reshape(2, 1, half)
    kv_bias = jnp.concatenate([jnp.zeros_like(halves), halves], 2)
    dma = pltpu.SemaphoreType.DMA
    return pl.pallas_call(
        functools.partial(fused_kernel, n),
        out_shape=jax.ShapeDtypeStruct((rows, depth), jnp.bfloat16),
        in_specs=[pl.BlockSpec(memory_space=pltpu.VMEM)] * 7,
        out_specs=pl.BlockSpec(memory_space=pltpu.VMEM),
        scratch_shapes=[
            pltpu.VMEM((rows, depth), jnp.bfloat16),
            pltpu.VMEM((2 * rows, depth), jnp.bfloat16),
            pltpu.VMEM((depth, 3 * half), jnp.bfloat16),
            pltpu.VMEM((lines, wrows, 3 * half), jnp.bfloat16),
            pltpu.VMEM((2 * lines, 2 * rows, 2 * half), jnp.bfloat16),
            pltpu.VMEM((heads, 2 * rows, HEAD_SIZE), jnp.bfloat16),
            pltpu.VMEM((heads, 2 * rows, 128), jnp.float32),
            pltpu.VMEM((heads, 2 * rows, 128), jnp.float32),
            pltpu.VMEM((heads, 2 * rows, HEAD_SIZE), jnp.float32),
            pltpu.VMEM((depth, width), jnp.bfloat16),
            pltpu.VMEM((2, 2 * rows, half), jnp.bfloat16),
            pltpu.VMEM((rows, width), jnp.bfloat16),
            dma((2,)),
            dma((2, lines)),
            dma((n,)),
            dma((n,)),
            dma((3, lines)),
            dma((lines,)),
            dma((3, lines)),
            dma((2 * lines,)),
            dma((3, lines)),
            dma((n,)),
            dma((n,)),
            dma((2,)),
        ],
        compiler_params=pltpu.CompilerParams(
            collective_id=0, has_side_effects=True, vmem_limit_bytes=48 * 2**20
        ),
    )(
        inputs,
        ln_gain.reshape(1, depth),
        ln_bias.reshape(1, depth),
        qkv_weight,
        kv_bias,
        out_weight,
        out_bias.reshape(1, depth),
    )


def per_device(inputs, ln_gain, ln_bias, qkv_weight, v_bias, out_weight, out_bias):
    n = lax.axis_size("tm")
    whole_tiles = (
        n % 4 == 0
        and qkv_weight.shape[0] % 16 == 0
        and out_weight.shape[1] == qkv_weight.shape[0]
        and inputs.shape[0] % 16 == 0
        and v_bias.shape[0] % (2 * HEAD_SIZE) == 0
    )
    arguments = (inputs, ln_gain, ln_bias, qkv_weight, v_bias, out_weight, out_bias)
    if whole_tiles:
        return per_device_fused(n, *arguments)
    return per_device_plain(*arguments)


def solution(mesh):
    return jax.shard_map(
        per_device,
        mesh=mesh,
        in_specs=(P(("groups", "tm"), None), P(), P(), P("tm", None), P(), P(None, "tm"), P()),
        out_specs=P(("groups", "tm"), None),
        check_vma=False,
    )
```

```python
import functools

import jax
import jax.numpy as jnp
from jax import lax
from jax.experimental import pallas as pl
from jax.experimental.pallas import tpu as pltpu
from jax.sharding import PartitionSpec as P

HEAD_SIZE = 64


def swapped(value, axis, apart):
    mask = 2**apart
    pairs = [(source, source ^ mask) for source in range(lax.axis_size(axis))]
    return lax.ppermute(value, axis, pairs)


def from_behind(block, axis, distance):
    devices = range(lax.axis_size(axis))
    route = [((i - distance) % len(devices), i) for i in devices]
    return lax.ppermute(block, axis, route)


def layer_norm(inputs, ln_gain, ln_bias):
    widened = inputs.astype(jnp.float32)
    average = jnp.mean(widened, -1, keepdims=True)
    centred = widened - average
    variance = jnp.mean(centred * centred, -1, keepdims=True)
    return (centred * lax.rsqrt(variance + 1e-05) * ln_gain + ln_bias).astype(jnp.bfloat16)


def attend(state_now, queries, key_part, value_part):
    running_max, running_sum, weighted = state_now
    key_count = key_part.shape[0]
    head_count = queries.shape[1]
    key_heads = key_part.reshape(key_count, head_count, HEAD_SIZE)
    value_heads = value_part.reshape(key_count, head_count, HEAD_SIZE)
    scores = jnp.einsum("qhd,khd->hqk", queries, key_heads, preferred_element_type=jnp.float32)
    new_max = jnp.maximum(running_max, jnp.max(scores, -1))
    rescale = jnp.exp(running_max - new_max)
    exponent = jnp.exp(scores - new_max[..., None])
    running_sum = running_sum * rescale + jnp.sum(exponent, -1)
    weights_bf = exponent.astype(jnp.bfloat16)
    weighted = weighted * rescale[..., None] + jnp.einsum(
        "hqk,khd->hqd", weights_bf, value_heads, preferred_element_type=jnp.float32
    )
    return (new_max, running_sum, weighted)


def empty_state(head_count, row_count):
    return (
        jnp.full((head_count, row_count), -jnp.inf, jnp.float32),
        jnp.zeros((head_count, row_count), jnp.float32),
        jnp.zeros((head_count, row_count, HEAD_SIZE), jnp.float32),
    )


def finish(final_state):
    mixed = final_state[2] / final_state[1][..., None]
    head_count, row_count = (mixed.shape[0], mixed.shape[1])
    return (
        jnp.transpose(mixed, (1, 0, 2))
        .reshape(row_count, head_count * HEAD_SIZE)
        .astype(jnp.bfloat16)
    )


def per_device_plain(inputs, ln_gain, ln_bias, qkv_weight, v_bias, out_weight, out_bias):
    normed = layer_norm(inputs, ln_gain, ln_bias)
    row_count = inputs.shape[0]
    head_width = v_bias.shape[0]
    head_count = head_width // HEAD_SIZE
    projected = jnp.dot(
        normed,
        lax.all_gather(qkv_weight, "tm", axis=0, tiled=True),
        preferred_element_type=jnp.float32,
    )
    queries = (projected[:, :head_width] * HEAD_SIZE ** (-0.5)).astype(jnp.bfloat16)
    key_rows = projected[:, head_width : 2 * head_width].astype(jnp.bfloat16)
    values = (projected[:, 2 * head_width :] + v_bias).astype(jnp.bfloat16)
    parity = lax.axis_index("tm") % 2
    half_count = head_count // 2
    half_width = half_count * HEAD_SIZE
    stacked = jnp.stack([queries, key_rows, values])
    keep_part = lax.dynamic_slice_in_dim(stacked, parity * half_width, half_width, 2)
    give_part = lax.dynamic_slice_in_dim(stacked, (1 - parity) * half_width, half_width, 2)
    got_part = swapped(give_part, "tm", 0)
    first_rows = jnp.where(parity == 0, keep_part, got_part)
    second_rows = jnp.where(parity == 0, got_part, keep_part)
    joined = jnp.concatenate([first_rows, second_rows], 1)
    pair_rows = 2 * row_count
    pair_queries = joined[0].reshape(pair_rows, half_count, HEAD_SIZE)
    key_value_block = joined[1:]
    state_now = attend(
        empty_state(half_count, pair_rows), pair_queries, key_value_block[0], key_value_block[1]
    )

    def cycle_turn(step, carry):
        state_now, block_now = carry
        block_now = from_behind(block_now, "tm", 2)
        return (attend(state_now, pair_queries, block_now[0], block_now[1]), block_now)

    final_state, unused_block = lax.fori_loop(
        0, lax.axis_size("tm") // 2 - 1, cycle_turn, (state_now, key_value_block)
    )
    pair_context = finish(final_state)
    mine_rows = lax.dynamic_slice_in_dim(pair_context, parity * row_count, row_count, 0)
    other_rows = lax.dynamic_slice_in_dim(pair_context, (1 - parity) * row_count, row_count, 0)
    back_rows = swapped(other_rows, "tm", 0)
    context = jnp.where(
        parity == 0,
        jnp.concatenate([mine_rows, back_rows], 1),
        jnp.concatenate([back_rows, mine_rows], 1),
    )
    projection = jnp.dot(
        context,
        lax.all_gather(out_weight, "tm", axis=1, tiled=True),
        preferred_element_type=jnp.float32,
    )
    return (inputs.astype(jnp.float32) + projection + out_bias).astype(jnp.bfloat16)


def fused_kernel(
    n,
    x_hbm, gain_hbm, bias_hbm, w_hbm, vb_hbm, wo_hbm, ob_hbm,
    o_ref,
    x_ref, gain_ref, bias_ref, w_ref, vb_ref, wo_ref, ob_ref, in_sem,
    xother, kv_bias, normed, wfull, wpass, kv, qh, top, total, acc, wofull, ctx, ctxfull,
    x_sem, w_send, w_core, w_across, w_recv, p_send, p_recv, kv_send, kv_recv, o_send, o_core, o_across, o_recv, c_sem,
):
    fetches = [
        pltpu.make_async_copy(source, target, in_sem.at[at])
        for at, (source, target) in enumerate(
            (
                (w_hbm, w_ref), (x_hbm, x_ref), (vb_hbm, vb_ref), (wo_hbm, wo_ref),
                (gain_hbm, gain_ref), (bias_hbm, bias_ref), (ob_hbm, ob_ref),
            )
        )
    ]
    for fetch in fetches:
        fetch.start()
    me = lax.axis_index("tm")
    lines = n // 4
    c = lax.rem(me, 2)
    y = lax.rem(lax.div(me, 2), 2)
    z = lax.div(me, 4)
    rows = x_ref.shape[0]
    wrows = w_ref.shape[0]
    width = wo_ref.shape[1]
    half = width // 2
    heads = half // HEAD_SIZE
    group = lax.axis_index("groups")
    side = lax.rem(group, 2)
    right, left = {"tm": me + 4}, {"tm": me - 4}
    has_right, has_left = z < lines - 1, z > 0
    other_y = {"tm": me + 2 - 4 * y}
    other_c = {"tm": me + 1 - 2 * c}
    other_x = {"groups": group + 1 - 2 * side}

    def send(src, dst, ssem, rsem, device):
        return pltpu.make_async_remote_copy(
            src_ref=src, dst_ref=dst, send_sem=ssem, recv_sem=rsem,
            device_id=device, device_id_type=pl.DeviceIdType.MESH,
        )

    def nth(t):
        near = jnp.minimum(z, lines - 1 - z)
        k = lax.div(t + 1, 2)
        both = jnp.where(lax.rem(t, 2) == 1, z - k, z + k)
        far = t - near
        one = jnp.where(z < lines - 1 - z, z + far, z - far)
        return jnp.where(t <= 2 * near, both, one)

    def w_block(zz, yy, cc):
        return zz * 4 + yy * 2 + cc

    def w_rows(ref, block):
        return ref.at[pl.ds(pl.multiple_of(block * wrows, wrows), wrows), :]

    def w_z(zz, way, device):
        b = w_block(zz, y, c)
        return send(w_rows(wfull, b), w_rows(wfull, b), w_send.at[way, zz], w_recv.at[b], device)

    def p_z(zz, way, device):
        return send(wpass.at[zz], wpass.at[zz], p_send.at[way, zz], p_recv.at[zz], device)

    def p_y(zz):
        b = w_block(zz, y, c)
        return send(wpass.at[zz], w_rows(wfull, b), p_send.at[2, zz], w_recv.at[b], other_y)

    def w_c(zz, yy, cc):
        b = w_block(zz, yy, cc)
        return send(w_rows(wfull, b), w_rows(wfull, b), w_core.at[b], w_recv.at[b], other_c)

    def w_x(zz, yy):
        b = w_block(zz, yy, c)
        return send(w_rows(wfull, b), w_rows(wfull, b), w_across.at[b], w_recv.at[b], other_x)

    def o_x(zz, yy):
        b = w_block(zz, yy, c)
        return send(w_rows(wofull, b), w_rows(wofull, b), o_across.at[b], o_recv.at[b], other_x)

    def carried(zz):
        return lax.rem(zz + side, 2) == 0

    def o_z(zz, way, device):
        b = w_block(zz, y, c)
        return send(w_rows(wofull, b), w_rows(wofull, b), o_send.at[way, zz], o_recv.at[b], device)

    def o_y(zz, yy):
        b = w_block(zz, yy, c)
        return send(w_rows(wofull, b), w_rows(wofull, b), o_send.at[2, zz], o_recv.at[b], other_y)

    def o_c(zz, yy, cc):
        b = w_block(zz, yy, cc)
        return send(w_rows(wofull, b), w_rows(wofull, b), o_core.at[b], o_recv.at[b], other_c)

    def kv_z(zz, way, device):
        b = zz * 2 + c
        return send(kv.at[b], kv.at[b], kv_send.at[way, zz], kv_recv.at[b], device)

    def kv_c(zz, cc):
        b = zz * 2 + cc
        return send(kv.at[b], kv.at[b], kv_send.at[2, zz], kv_recv.at[b], other_c)

    def along(zz, makers):
        @pl.when(jnp.logical_and(zz <= z, has_right))
        def _():
            for maker in makers:
                maker(zz, 0, right).start()

        @pl.when(jnp.logical_and(zz >= z, has_left))
        def _():
            for maker in makers:
                maker(zz, 1, left).start()

    def along_done(zz, makers):
        @pl.when(jnp.logical_and(zz <= z, has_right))
        def _():
            for maker in makers:
                maker(zz, 0, right).wait_send()

        @pl.when(jnp.logical_and(zz >= z, has_left))
        def _():
            for maker in makers:
                maker(zz, 1, left).wait_send()

    barrier = pltpu.get_barrier_semaphore()

    def greet(device):
        pl.semaphore_signal(barrier, inc=1, device_id=device, device_id_type=pl.DeviceIdType.MESH)

    greet(other_y)
    greet(other_c)
    greet(other_x)

    @pl.when(has_right)
    def _():
        greet(right)

    @pl.when(has_left)
    def _():
        greet(left)

    kv_bias[...] = jnp.zeros_like(kv_bias)
    fetches[0].wait()
    fetches[2].wait()
    mine = pl.ds(pl.multiple_of(me * wrows, wrows), wrows)
    for yy in range(2):

        @pl.when(y == yy)
        def _():
            kv_bias[:, half:] = vb_ref[yy * half : (yy + 1) * half].reshape(1, half)
            for at, part in enumerate((1, 2, 0)):
                wide = pl.ds(at * half, half)
                wfull[mine, wide] = w_ref[:, pl.ds(part * width + yy * half, half)]
                wpass[z, :, wide] = w_ref[:, pl.ds(part * width + (1 - yy) * half, half)]

    peers = 3 + jnp.where(has_right, 1, 0) + jnp.where(has_left, 1, 0)
    pl.semaphore_wait(barrier, peers)

    @pl.when(carried(z))
    def _():
        along(z, (p_z,))
        p_y(z).start()

    @pl.when(jnp.logical_not(carried(z)))
    def _():
        along(z, (w_z,))

    fetches[1].wait()
    x_copy = send(x_ref, xother, x_sem.at[0], x_sem.at[1], other_y)
    x_copy.start()
    w_c(z, y, c).start()
    for fetch in fetches[3:]:
        fetch.wait()
    wofull[mine, :] = wo_ref[...]

    def norm_rows(ref, yy):
        widened = ref[...].astype(jnp.float32)
        average = jnp.mean(widened, -1, keepdims=True)
        centred = widened - average
        variance = jnp.mean(centred * centred, -1, keepdims=True)
        normed[pl.ds(pl.multiple_of(yy * rows, rows), rows), :] = (
            centred * lax.rsqrt(variance + 1e-05) * gain_ref[...] + bias_ref[...]
        ).astype(jnp.bfloat16)

    norm_rows(x_ref, y)

    def w_turn(t, carry):
        zz = nth(t)

        @pl.when(jnp.logical_and(t < lines, carried(zz)))
        def _():
            p_z(zz, 0, right).wait_recv()
            along(zz, (p_z,))
            p_y(zz).start()

        @pl.when(jnp.logical_and(t < lines, jnp.logical_not(carried(zz))))
        def _():
            w_z(zz, 0, right).wait_recv()
            along(zz, (w_z,))
            w_x(zz, y).start()
            w_c(zz, y, c).start()

        first = nth(t - 1)

        @pl.when(jnp.logical_and(t <= lines, carried(first)))
        def _():
            @pl.when(t > 1)
            def _():
                w_x(first, y).wait_recv()
                w_c(first, y, c).start()

            w_x(first, 1 - y).wait_recv()
            w_x(first, 1 - y).start()
            w_c(first, 1 - y, c).start()

        second = nth(t - 2)

        @pl.when(jnp.logical_and(t > 1, jnp.logical_not(carried(second))))
        def _():
            w_x(second, 1 - y).wait_recv()
            w_c(second, 1 - y, c).start()

        return carry

    lax.fori_loop(1, lines + 2, w_turn, 0)

    @pl.when(carried(z))
    def _():
        along(z, (o_z,))
        o_y(z, y).start()

    o_c(z, y, c).start()

    def o_turn(t):
        zz = nth(t)

        @pl.when(jnp.logical_and(t < lines, carried(zz)))
        def _():
            o_z(zz, 0, right).wait_recv()
            along(zz, (o_z,))
            o_y(zz, y).start()
            o_x(zz, y).start()
            o_c(zz, y, c).start()

        first = nth(t - 1)

        @pl.when(jnp.logical_and(t <= lines, carried(first)))
        def _():
            o_x(first, 1 - y).wait_recv()
            o_x(first, 1 - y).start()
            o_c(first, 1 - y, c).start()

        @pl.when(jnp.logical_and(jnp.logical_and(t > 1, t <= lines), jnp.logical_not(carried(first))))
        def _():
            o_x(first, y).wait_recv()
            o_c(first, y, c).start()

        second = nth(t - 2)

        @pl.when(jnp.logical_and(t > 1, jnp.logical_not(carried(second))))
        def _():
            o_x(second, 1 - y).wait_recv()
            o_c(second, 1 - y, c).start()

    x_copy.wait()
    norm_rows(xother, 1 - y)

    def w_arrived(zz, carry):
        for yy in range(2):
            w_c(zz, yy, 1 - c).wait_recv()
        return carry

    lax.fori_loop(0, lines, w_arrived, 0)

    own = z * 2 + c
    both = normed[...]
    kv[own] = (
        jnp.dot(both, wfull[:, : 2 * half], preferred_element_type=jnp.float32) + kv_bias[...]
    ).astype(jnp.bfloat16)
    along(z, (kv_z,))
    kv_c(z, c).start()
    queries = (
        jnp.dot(both, wfull[:, 2 * half :], preferred_element_type=jnp.float32) * HEAD_SIZE ** (-0.5)
    ).astype(jnp.bfloat16)
    for h in range(heads):
        qh[h] = queries[:, h * HEAD_SIZE : (h + 1) * HEAD_SIZE]
    top[...] = jnp.full_like(top, -jnp.inf)
    total[...] = jnp.zeros_like(total)
    acc[...] = jnp.zeros_like(acc)

    def attend_block(b):
        for h in range(heads):
            key_part = kv[b, :, h * HEAD_SIZE : (h + 1) * HEAD_SIZE]
            value_part = kv[b, :, half + h * HEAD_SIZE : half + (h + 1) * HEAD_SIZE]
            scores = lax.dot_general(
                qh[h], key_part, (((1,), (1,)), ((), ())), preferred_element_type=jnp.float32
            )
            old_top = top[h]
            new_top = jnp.maximum(old_top, jnp.max(scores, -1, keepdims=True))
            rescale = jnp.exp(old_top - new_top)
            exponent = jnp.exp(scores - new_top[:, :1])
            total[h] = total[h] * rescale + jnp.sum(exponent, -1, keepdims=True)
            top[h] = new_top
            acc[h] = acc[h] * rescale[:, :HEAD_SIZE] + jnp.dot(
                exponent.astype(jnp.bfloat16), value_part, preferred_element_type=jnp.float32
            )

    def kv_turn(t, carry):
        zz = nth(t)

        @pl.when(t > 0)
        def _():
            kv_z(zz, 0, right).wait_recv()
            along(zz, (kv_z,))
            kv_c(zz, c).start()

        attend_block(zz * 2 + c)

        @pl.when(t > 0)
        def _():
            o_turn(t)

        kv_c(zz, 1 - c).wait_recv()
        attend_block(zz * 2 + 1 - c)
        return carry

    lax.fori_loop(0, lines, kv_turn, 0)

    for h in range(heads):
        ctx[y, :, h * HEAD_SIZE : (h + 1) * HEAD_SIZE] = (
            acc[h] / total[h][:, :HEAD_SIZE]
        ).astype(jnp.bfloat16)
    theirs = pl.ds(pl.multiple_of((1 - y) * rows, rows), rows)
    ours = pl.ds(pl.multiple_of(y * rows, rows), rows)
    c_copy = send(ctx.at[y, theirs, :], ctx.at[y, theirs, :], c_sem.at[0], c_sem.at[1], other_y)
    c_back = send(ctx.at[1 - y, ours, :], ctx.at[1 - y, ours, :], c_sem.at[0], c_sem.at[1], other_y)
    c_copy.start()
    o_turn(jnp.int32(lines))
    o_turn(jnp.int32(lines + 1))

    def drained(zz, carry):
        @pl.when(carried(zz))
        def _():
            along_done(zz, (p_z, o_z))
            p_y(zz).wait_send()
            o_y(zz, y).wait_send()
            w_x(zz, 1 - y).wait_send()
            o_x(zz, 1 - y).wait_send()

            @pl.when(zz != z)
            def _():
                o_x(zz, y).wait_send()

        @pl.when(jnp.logical_not(carried(zz)))
        def _():
            along_done(zz, (w_z,))

            @pl.when(zz != z)
            def _():
                w_x(zz, y).wait_send()

        along_done(zz, (kv_z,))
        kv_c(zz, c).wait_send()
        for yy in range(2):
            w_c(zz, yy, c).wait_send()
            o_c(zz, yy, c).wait_send()
            o_c(zz, yy, 1 - c).wait_recv()
        return carry

    lax.fori_loop(0, lines, drained, 0)
    c_copy.wait_send()
    c_back.wait_recv()
    for part in range(2):
        ctxfull[:, part * half : (part + 1) * half] = ctx[part, ours, :]
    projection = lax.dot_general(
        ctxfull[...], wofull[...], (((1,), (1,)), ((), ())), preferred_element_type=jnp.float32
    )
    o_ref[...] = (x_ref[...].astype(jnp.float32) + projection + ob_ref[...]).astype(o_ref.dtype)


def per_device_fused(n, inputs, ln_gain, ln_bias, qkv_weight, v_bias, out_weight, out_bias):
    rows, depth = inputs.shape
    width = v_bias.shape[0]
    half = width // 2
    heads = half // HEAD_SIZE
    lines = n // 4
    wrows = qkv_weight.shape[0]
    dma = pltpu.SemaphoreType.DMA
    return pl.pallas_call(
        functools.partial(fused_kernel, n),
        out_shape=jax.ShapeDtypeStruct((rows, depth), jnp.bfloat16),
        in_specs=[pl.BlockSpec(memory_space=pltpu.HBM)] * 7,
        out_specs=pl.BlockSpec(memory_space=pltpu.VMEM),
        scratch_shapes=[
            pltpu.VMEM((rows, depth), jnp.bfloat16),
            pltpu.VMEM((depth,), jnp.float32),
            pltpu.VMEM((depth,), jnp.float32),
            pltpu.VMEM(qkv_weight.shape, jnp.bfloat16),
            pltpu.VMEM((width,), jnp.float32),
            pltpu.VMEM((wrows, width), jnp.bfloat16),
            pltpu.VMEM((depth,), jnp.float32),
            dma((7,)),
            pltpu.VMEM((rows, depth), jnp.bfloat16),
            pltpu.VMEM((1, 2 * half), jnp.float32),
            pltpu.VMEM((2 * rows, depth), jnp.bfloat16),
            pltpu.VMEM((depth, 3 * half), jnp.bfloat16),
            pltpu.VMEM((lines, wrows, 3 * half), jnp.bfloat16),
            pltpu.VMEM((2 * lines, 2 * rows, 2 * half), jnp.bfloat16),
            pltpu.VMEM((heads, 2 * rows, HEAD_SIZE), jnp.bfloat16),
            pltpu.VMEM((heads, 2 * rows, 128), jnp.float32),
            pltpu.VMEM((heads, 2 * rows, 128), jnp.float32),
            pltpu.VMEM((heads, 2 * rows, HEAD_SIZE), jnp.float32),
            pltpu.VMEM((depth, width), jnp.bfloat16),
            pltpu.VMEM((2, 2 * rows, half), jnp.bfloat16),
            pltpu.VMEM((rows, width), jnp.bfloat16),
            dma((2,)),
            dma((2, lines)),
            dma((n,)),
            dma((n,)),
            dma((n,)),
            dma((3, lines)),
            dma((lines,)),
            dma((3, lines)),
            dma((2 * lines,)),
            dma((3, lines)),
            dma((n,)),
            dma((n,)),
            dma((n,)),
            dma((2,)),
        ],
        compiler_params=pltpu.CompilerParams(
            collective_id=0, has_side_effects=True, vmem_limit_bytes=48 * 2**20
        ),
    )(inputs, ln_gain, ln_bias, qkv_weight, v_bias, out_weight.T, out_bias)


def per_device(inputs, ln_gain, ln_bias, qkv_weight, v_bias, out_weight, out_bias):
    n = lax.axis_size("tm")
    whole_tiles = (
        n % 4 == 0
        and lax.axis_size("groups") % 2 == 0
        and qkv_weight.shape[0] % 16 == 0
        and out_weight.shape[1] == qkv_weight.shape[0]
        and inputs.shape[0] % 16 == 0
        and v_bias.shape[0] % (2 * HEAD_SIZE) == 0
    )
    arguments = (inputs, ln_gain, ln_bias, qkv_weight, v_bias, out_weight, out_bias)
    if whole_tiles:
        return per_device_fused(n, *arguments)
    return per_device_plain(*arguments)


def solution(mesh):
    return jax.shard_map(
        per_device,
        mesh=mesh,
        in_specs=(P(("groups", "tm"), None), P(), P(), P("tm", None), P(), P(None, "tm"), P()),
        out_specs=P(("groups", "tm"), None),
        check_vma=False,
    )
```

```python
import functools

import jax
import jax.numpy as jnp
from jax import lax
from jax.experimental import pallas as pl
from jax.experimental.pallas import tpu as pltpu
from jax.sharding import PartitionSpec as P

HEAD_SIZE = 64


def swapped(value, axis, apart):
    mask = 2**apart
    pairs = [(source, source ^ mask) for source in range(lax.axis_size(axis))]
    return lax.ppermute(value, axis, pairs)


def from_behind(block, axis, distance):
    devices = range(lax.axis_size(axis))
    route = [((i - distance) % len(devices), i) for i in devices]
    return lax.ppermute(block, axis, route)


def layer_norm(inputs, ln_gain, ln_bias):
    widened = inputs.astype(jnp.float32)
    average = jnp.mean(widened, -1, keepdims=True)
    centred = widened - average
    variance = jnp.mean(centred * centred, -1, keepdims=True)
    return (centred * lax.rsqrt(variance + 1e-05) * ln_gain + ln_bias).astype(jnp.bfloat16)


def attend(state_now, queries, key_part, value_part):
    running_max, running_sum, weighted = state_now
    key_count = key_part.shape[0]
    head_count = queries.shape[1]
    key_heads = key_part.reshape(key_count, head_count, HEAD_SIZE)
    value_heads = value_part.reshape(key_count, head_count, HEAD_SIZE)
    scores = jnp.einsum("qhd,khd->hqk", queries, key_heads, preferred_element_type=jnp.float32)
    new_max = jnp.maximum(running_max, jnp.max(scores, -1))
    rescale = jnp.exp(running_max - new_max)
    exponent = jnp.exp(scores - new_max[..., None])
    running_sum = running_sum * rescale + jnp.sum(exponent, -1)
    weights_bf = exponent.astype(jnp.bfloat16)
    weighted = weighted * rescale[..., None] + jnp.einsum(
        "hqk,khd->hqd", weights_bf, value_heads, preferred_element_type=jnp.float32
    )
    return (new_max, running_sum, weighted)


def empty_state(head_count, row_count):
    return (
        jnp.full((head_count, row_count), -jnp.inf, jnp.float32),
        jnp.zeros((head_count, row_count), jnp.float32),
        jnp.zeros((head_count, row_count, HEAD_SIZE), jnp.float32),
    )


def finish(final_state):
    mixed = final_state[2] / final_state[1][..., None]
    head_count, row_count = (mixed.shape[0], mixed.shape[1])
    return (
        jnp.transpose(mixed, (1, 0, 2))
        .reshape(row_count, head_count * HEAD_SIZE)
        .astype(jnp.bfloat16)
    )


def per_device_plain(inputs, ln_gain, ln_bias, qkv_weight, v_bias, out_weight, out_bias):
    normed = layer_norm(inputs, ln_gain, ln_bias)
    row_count = inputs.shape[0]
    head_width = v_bias.shape[0]
    head_count = head_width // HEAD_SIZE
    projected = jnp.dot(
        normed,
        lax.all_gather(qkv_weight, "tm", axis=0, tiled=True),
        preferred_element_type=jnp.float32,
    )
    queries = (projected[:, :head_width] * HEAD_SIZE ** (-0.5)).astype(jnp.bfloat16)
    key_rows = projected[:, head_width : 2 * head_width].astype(jnp.bfloat16)
    values = (projected[:, 2 * head_width :] + v_bias).astype(jnp.bfloat16)
    parity = lax.axis_index("tm") % 2
    half_count = head_count // 2
    half_width = half_count * HEAD_SIZE
    stacked = jnp.stack([queries, key_rows, values])
    keep_part = lax.dynamic_slice_in_dim(stacked, parity * half_width, half_width, 2)
    give_part = lax.dynamic_slice_in_dim(stacked, (1 - parity) * half_width, half_width, 2)
    got_part = swapped(give_part, "tm", 0)
    first_rows = jnp.where(parity == 0, keep_part, got_part)
    second_rows = jnp.where(parity == 0, got_part, keep_part)
    joined = jnp.concatenate([first_rows, second_rows], 1)
    pair_rows = 2 * row_count
    pair_queries = joined[0].reshape(pair_rows, half_count, HEAD_SIZE)
    key_value_block = joined[1:]
    state_now = attend(
        empty_state(half_count, pair_rows), pair_queries, key_value_block[0], key_value_block[1]
    )

    def cycle_turn(step, carry):
        state_now, block_now = carry
        block_now = from_behind(block_now, "tm", 2)
        return (attend(state_now, pair_queries, block_now[0], block_now[1]), block_now)

    final_state, unused_block = lax.fori_loop(
        0, lax.axis_size("tm") // 2 - 1, cycle_turn, (state_now, key_value_block)
    )
    pair_context = finish(final_state)
    mine_rows = lax.dynamic_slice_in_dim(pair_context, parity * row_count, row_count, 0)
    other_rows = lax.dynamic_slice_in_dim(pair_context, (1 - parity) * row_count, row_count, 0)
    back_rows = swapped(other_rows, "tm", 0)
    context = jnp.where(
        parity == 0,
        jnp.concatenate([mine_rows, back_rows], 1),
        jnp.concatenate([back_rows, mine_rows], 1),
    )
    projection = jnp.dot(
        context,
        lax.all_gather(out_weight, "tm", axis=1, tiled=True),
        preferred_element_type=jnp.float32,
    )
    return (inputs.astype(jnp.float32) + projection + out_bias).astype(jnp.bfloat16)


def fused_kernel(
    n,
    x_hbm, gain_hbm, bias_hbm, w_hbm, vb_hbm, wo_hbm, ob_hbm,
    o_ref,
    x_ref, gain_ref, bias_ref, w_ref, vb_ref, wo_ref, ob_ref, in_sem,
    xother, kv_bias, normed, wkv, wq, pass_kv, pass_q, kv, qh, top, total, acc, wofull, ctx, ctxfull,
    x_sem, wkv_send, wkv_recv, wq_send, wq_recv, kv_send, kv_recv, o_send, o_recv, c_sem,
):
    fetches = [
        pltpu.make_async_copy(source, target, in_sem.at[at])
        for at, (source, target) in enumerate(
            (
                (w_hbm, w_ref), (x_hbm, x_ref), (vb_hbm, vb_ref), (wo_hbm, wo_ref),
                (gain_hbm, gain_ref), (bias_hbm, bias_ref), (ob_hbm, ob_ref),
            )
        )
    ]
    for fetch in fetches:
        fetch.start()
    me = lax.axis_index("tm")
    lines = n // 4
    c = lax.rem(me, 2)
    y = lax.rem(lax.div(me, 2), 2)
    z = lax.div(me, 4)
    rows = x_ref.shape[0]
    wrows = w_ref.shape[0]
    width = wo_ref.shape[1]
    half = width // 2
    heads = half // HEAD_SIZE
    group = lax.axis_index("groups")
    side = lax.rem(group, 2)
    right, left = {"tm": me + 4}, {"tm": me - 4}
    has_right, has_left = z < lines - 1, z > 0
    other_y = {"tm": me + 2 - 4 * y}
    other_c = {"tm": me + 1 - 2 * c}
    other_x = {"groups": group + 1 - 2 * side}

    def send(src, dst, ssem, rsem, device):
        return pltpu.make_async_remote_copy(
            src_ref=src, dst_ref=dst, send_sem=ssem, recv_sem=rsem,
            device_id=device, device_id_type=pl.DeviceIdType.MESH,
        )

    def nth(t):
        near = jnp.minimum(z, lines - 1 - z)
        k = lax.div(t + 1, 2)
        both = jnp.where(lax.rem(t, 2) == 1, z - k, z + k)
        far = t - near
        one = jnp.where(z < lines - 1 - z, z + far, z - far)
        return jnp.where(t <= 2 * near, both, one)

    relayed = jnp.where(side == 0, y, 1 - y)

    def block_of(zz, yy, cc):
        return zz * 4 + yy * 2 + cc

    def block_rows(ref, block):
        return ref.at[pl.ds(pl.multiple_of(block * wrows, wrows), wrows), :]

    class Stream:
        def __init__(self, ref, ssem, rsem):
            self.ref, self.ssem, self.rsem = ref, ssem, rsem

        def copy(self, way, slot, zz, yy, cc, device, source=None):
            b = block_of(zz, yy, cc)
            there = block_rows(self.ref, b)
            return send(
                there if source is None else source, there, self.ssem.at[way, slot], self.rsem.at[b], device
            )

        def to_z(self, zz, yy):
            return self.copy(0, zz, z, yy, c, {"tm": block_of(zz, y, c)})

        def to_y(self, zz, source=None):
            return self.copy(1, zz, zz, y, c, other_y, source)

        def to_x(self, zz, yy):
            return self.copy(2, zz * 2 + yy, zz, yy, c, other_x)

        def to_c(self, zz, yy):
            return self.copy(3, zz * 2 + yy, zz, yy, c, other_c)

        def arrived(self, zz, yy, cc):
            self.copy(3, 0, zz, yy, cc, other_c).wait_recv()

    keys_values = Stream(wkv, wkv_send, wkv_recv)
    query_part = Stream(wq, wq_send, wq_recv)
    out_part = Stream(wofull, o_send, o_recv)

    def carried(zz):
        return lax.rem(zz + side, 2) == 0

    def each_other(act):
        def turn(t, carry):
            act(nth(t))
            return carry

        lax.fori_loop(1, lines, turn, 0)

    def each(act):
        def turn(zz, carry):
            act(zz)
            return carry

        lax.fori_loop(0, lines, turn, 0)

    def kv_z(zz, way, device):
        b = zz * 2 + c
        return send(kv.at[b], kv.at[b], kv_send.at[way, zz], kv_recv.at[b], device)

    def kv_c(zz, cc):
        b = zz * 2 + cc
        return send(kv.at[b], kv.at[b], kv_send.at[2, zz], kv_recv.at[b], other_c)

    def along(zz, makers):
        @pl.when(jnp.logical_and(zz <= z, has_right))
        def _():
            for maker in makers:
                maker(zz, 0, right).start()

        @pl.when(jnp.logical_and(zz >= z, has_left))
        def _():
            for maker in makers:
                maker(zz, 1, left).start()

    def along_done(zz, makers):
        @pl.when(jnp.logical_and(zz <= z, has_right))
        def _():
            for maker in makers:
                maker(zz, 0, right).wait_send()

        @pl.when(jnp.logical_and(zz >= z, has_left))
        def _():
            for maker in makers:
                maker(zz, 1, left).wait_send()

    barrier = pltpu.get_barrier_semaphore()

    def greet(device):
        pl.semaphore_signal(barrier, inc=1, device_id=device, device_id_type=pl.DeviceIdType.MESH)

    greet(other_y)
    greet(other_c)
    greet(other_x)
    each_other(lambda zz: greet({"tm": block_of(zz, y, c)}))

    kv_bias[...] = jnp.zeros_like(kv_bias)
    fetches[0].wait()
    fetches[2].wait()
    mine = pl.ds(pl.multiple_of(me * wrows, wrows), wrows)
    for yy in range(2):

        @pl.when(y == yy)
        def _():
            kv_bias[:, half:] = vb_ref[yy * half : (yy + 1) * half].reshape(1, half)
            for at, part in enumerate((1, 2)):
                wide = pl.ds(at * half, half)
                wkv[mine, wide] = w_ref[:, pl.ds(part * width + yy * half, half)]
                pass_kv[:, wide] = w_ref[:, pl.ds(part * width + (1 - yy) * half, half)]
            wq[mine, :half] = w_ref[:, pl.ds(yy * half, half)]
            pass_q[:, :half] = w_ref[:, pl.ds((1 - yy) * half, half)]

    pl.semaphore_wait(barrier, lines + 2)

    pairs = ((keys_values, pass_kv), (query_part, pass_q))
    for stream, passed in pairs:
        stream.to_y(z, passed).start()

        @pl.when(side == 0)
        def _():
            each_other(lambda zz: stream.to_z(zz, y).start())

        stream.to_c(z, y).start()

    fetches[1].wait()
    x_copy = send(x_ref, xother, x_sem.at[0], x_sem.at[1], other_y)
    x_copy.start()
    for fetch in fetches[3:]:
        fetch.wait()
    wofull[mine, :] = wo_ref[...]

    def norm_rows(ref, yy):
        widened = ref[...].astype(jnp.float32)
        average = jnp.mean(widened, -1, keepdims=True)
        centred = widened - average
        variance = jnp.mean(centred * centred, -1, keepdims=True)
        normed[pl.ds(pl.multiple_of(yy * rows, rows), rows), :] = (
            centred * lax.rsqrt(variance + 1e-05) * gain_ref[...] + bias_ref[...]
        ).astype(jnp.bfloat16)

    norm_rows(x_ref, y)

    for stream, passed in pairs:
        stream.arrived(z, 1 - y, c)

        @pl.when(side == 1)
        def _():
            each_other(lambda zz: stream.to_z(zz, 1 - y).start())

        stream.to_c(z, 1 - y).start()

    @pl.when(carried(z))
    def _():
        each_other(lambda zz: out_part.to_z(zz, y).start())
        out_part.to_y(z).start()

    out_part.to_c(z, y).start()

    def spread(stream):
        def turn(t, carry):
            @pl.when(t < lines)
            def _():
                zz = nth(t)
                stream.arrived(zz, relayed, c)
                stream.to_x(zz, relayed).start()
                stream.to_c(zz, relayed).start()

            @pl.when(t > 1)
            def _():
                before = nth(t - 1)
                stream.arrived(before, 1 - relayed, c)
                stream.to_c(before, 1 - relayed).start()

            return carry

        lax.fori_loop(1, lines + 1, turn, 0)

    def gathered(stream):
        def act(zz):
            for yy in range(2):
                stream.arrived(zz, yy, 1 - c)

        each(act)

    spread(keys_values)
    x_copy.wait()
    norm_rows(xother, 1 - y)
    gathered(keys_values)

    def out_first(zz):
        @pl.when(carried(zz))
        def _():
            out_part.arrived(zz, y, c)
            out_part.to_y(zz).start()
            out_part.to_x(zz, y).start()
            out_part.to_c(zz, y).start()

    def out_second(zz):
        @pl.when(carried(zz))
        def _():
            out_part.arrived(zz, 1 - y, c)
            out_part.to_x(zz, 1 - y).start()
            out_part.to_c(zz, 1 - y).start()

        @pl.when(jnp.logical_and(zz != z, jnp.logical_not(carried(zz))))
        def _():
            out_part.arrived(zz, y, c)
            out_part.to_c(zz, y).start()

    def out_third(zz):
        @pl.when(jnp.logical_not(carried(zz)))
        def _():
            out_part.arrived(zz, 1 - y, c)
            out_part.to_c(zz, 1 - y).start()

    own = z * 2 + c
    both = normed[...]
    kv[own] = (
        jnp.dot(both, wkv[...], preferred_element_type=jnp.float32) + kv_bias[...]
    ).astype(jnp.bfloat16)
    along(z, (kv_z,))
    kv_c(z, c).start()
    spread(query_part)
    gathered(query_part)
    queries = (
        jnp.dot(both, wq[:, :half], preferred_element_type=jnp.float32) * HEAD_SIZE ** (-0.5)
    ).astype(jnp.bfloat16)
    for h in range(heads):
        qh[h] = queries[:, h * HEAD_SIZE : (h + 1) * HEAD_SIZE]
    top[...] = jnp.full_like(top, -jnp.inf)
    total[...] = jnp.zeros_like(total)
    acc[...] = jnp.zeros_like(acc)

    def attend_block(b):
        for h in range(heads):
            key_part = kv[b, :, h * HEAD_SIZE : (h + 1) * HEAD_SIZE]
            value_part = kv[b, :, half + h * HEAD_SIZE : half + (h + 1) * HEAD_SIZE]
            scores = lax.dot_general(
                qh[h], key_part, (((1,), (1,)), ((), ())), preferred_element_type=jnp.float32
            )
            old_top = top[h]
            new_top = jnp.maximum(old_top, jnp.max(scores, -1, keepdims=True))
            rescale = jnp.exp(old_top - new_top)
            exponent = jnp.exp(scores - new_top[:, :1])
            total[h] = total[h] * rescale + jnp.sum(exponent, -1, keepdims=True)
            top[h] = new_top
            acc[h] = acc[h] * rescale[:, :HEAD_SIZE] + jnp.dot(
                exponent.astype(jnp.bfloat16), value_part, preferred_element_type=jnp.float32
            )

    def kv_turn(t, carry):
        zz = nth(t)

        @pl.when(t > 0)
        def _():
            kv_z(zz, 0, right).wait_recv()
            along(zz, (kv_z,))
            kv_c(zz, c).start()

        attend_block(zz * 2 + c)
        kv_c(zz, 1 - c).wait_recv()
        attend_block(zz * 2 + 1 - c)

        @pl.when(t == 0)
        def _():
            each(out_second)

        @pl.when(t == min(1, lines - 1))
        def _():
            each(out_third)

        return carry

    each_other(out_first)
    lax.fori_loop(0, lines, kv_turn, 0)

    for h in range(heads):
        ctx[y, :, h * HEAD_SIZE : (h + 1) * HEAD_SIZE] = (
            acc[h] / total[h][:, :HEAD_SIZE]
        ).astype(jnp.bfloat16)
    theirs = pl.ds(pl.multiple_of((1 - y) * rows, rows), rows)
    ours = pl.ds(pl.multiple_of(y * rows, rows), rows)
    c_copy = send(ctx.at[y, theirs, :], ctx.at[y, theirs, :], c_sem.at[0], c_sem.at[1], other_y)
    c_back = send(ctx.at[1 - y, ours, :], ctx.at[1 - y, ours, :], c_sem.at[0], c_sem.at[1], other_y)
    c_copy.start()

    def drained(zz, carry):
        for stream, passed in pairs:
            for yy in range(2):
                stream.to_c(zz, yy).wait_send()

            @pl.when(zz != z)
            def _():
                stream.to_z(zz, relayed).wait_send()
                stream.to_x(zz, relayed).wait_send()

        for yy in range(2):
            out_part.to_c(zz, yy).wait_send()
            out_part.arrived(zz, yy, 1 - c)

        @pl.when(carried(zz))
        def _():
            out_part.to_y(zz).wait_send()
            out_part.to_x(zz, 1 - y).wait_send()

            @pl.when(zz != z)
            def _():
                out_part.to_x(zz, y).wait_send()

        @pl.when(jnp.logical_and(zz != z, carried(z)))
        def _():
            out_part.to_z(zz, y).wait_send()

        along_done(zz, (kv_z,))
        kv_c(zz, c).wait_send()
        return carry

    for stream, passed in pairs:
        stream.to_y(z, passed).wait_send()
    lax.fori_loop(0, lines, drained, 0)
    c_copy.wait_send()
    c_back.wait_recv()
    for part in range(2):
        ctxfull[:, part * half : (part + 1) * half] = ctx[part, ours, :half]
    projection = lax.dot_general(
        ctxfull[...], wofull[...], (((1,), (1,)), ((), ())), preferred_element_type=jnp.float32
    )
    o_ref[...] = (x_ref[...].astype(jnp.float32) + projection + ob_ref[...]).astype(o_ref.dtype)


def per_device_fused(n, inputs, ln_gain, ln_bias, qkv_weight, v_bias, out_weight, out_bias):
    rows, depth = inputs.shape
    width = v_bias.shape[0]
    half = width // 2
    heads = half // HEAD_SIZE
    lines = n // 4
    wrows = qkv_weight.shape[0]
    wide = pl.cdiv(half, 128) * 128
    dma = pltpu.SemaphoreType.DMA
    return pl.pallas_call(
        functools.partial(fused_kernel, n),
        out_shape=jax.ShapeDtypeStruct((rows, depth), jnp.bfloat16),
        in_specs=[pl.BlockSpec(memory_space=pltpu.HBM)] * 7,
        out_specs=pl.BlockSpec(memory_space=pltpu.VMEM),
        scratch_shapes=[
            pltpu.VMEM((rows, depth), jnp.bfloat16),
            pltpu.VMEM((depth,), jnp.float32),
            pltpu.VMEM((depth,), jnp.float32),
            pltpu.VMEM(qkv_weight.shape, jnp.bfloat16),
            pltpu.VMEM((width,), jnp.float32),
            pltpu.VMEM((wrows, width), jnp.bfloat16),
            pltpu.VMEM((depth,), jnp.float32),
            dma((7,)),
            pltpu.VMEM((rows, depth), jnp.bfloat16),
            pltpu.VMEM((1, 2 * half), jnp.float32),
            pltpu.VMEM((2 * rows, depth), jnp.bfloat16),
            pltpu.VMEM((depth, 2 * half), jnp.bfloat16),
            pltpu.VMEM((depth, wide), jnp.bfloat16),
            pltpu.VMEM((wrows, 2 * half), jnp.bfloat16),
            pltpu.VMEM((wrows, wide), jnp.bfloat16),
            pltpu.VMEM((2 * lines, 2 * rows, 2 * half), jnp.bfloat16),
            pltpu.VMEM((heads, 2 * rows, HEAD_SIZE), jnp.bfloat16),
            pltpu.VMEM((heads, 2 * rows, 128), jnp.float32),
            pltpu.VMEM((heads, 2 * rows, 128), jnp.float32),
            pltpu.VMEM((heads, 2 * rows, HEAD_SIZE), jnp.float32),
            pltpu.VMEM((depth, width), jnp.bfloat16),
            pltpu.VMEM((2, 2 * rows, wide), jnp.bfloat16),
            pltpu.VMEM((rows, width), jnp.bfloat16),
            dma((2,)),
            dma((4, 2 * lines)),
            dma((n,)),
            dma((4, 2 * lines)),
            dma((n,)),
            dma((3, lines)),
            dma((2 * lines,)),
            dma((4, 2 * lines)),
            dma((n,)),
            dma((2,)),
        ],
        compiler_params=pltpu.CompilerParams(
            collective_id=0, has_side_effects=True, vmem_limit_bytes=62 * 2**20
        ),
    )(inputs, ln_gain, ln_bias, qkv_weight, v_bias, out_weight.T, out_bias)


def per_device(inputs, ln_gain, ln_bias, qkv_weight, v_bias, out_weight, out_bias):
    n = lax.axis_size("tm")
    whole_tiles = (
        n % 4 == 0
        and lax.axis_size("groups") % 2 == 0
        and qkv_weight.shape[0] % 16 == 0
        and out_weight.shape[1] == qkv_weight.shape[0]
        and inputs.shape[0] % 16 == 0
        and v_bias.shape[0] % (2 * HEAD_SIZE) == 0
    )
    arguments = (inputs, ln_gain, ln_bias, qkv_weight, v_bias, out_weight, out_bias)
    if whole_tiles:
        return per_device_fused(n, *arguments)
    return per_device_plain(*arguments)


def solution(mesh):
    return jax.shard_map(
        per_device,
        mesh=mesh,
        in_specs=(P(("groups", "tm"), None), P(), P(), P("tm", None), P(), P(None, "tm"), P()),
        out_specs=P(("groups", "tm"), None),
        check_vma=False,
    )
```

```python
import functools

import jax
import jax.numpy as jnp
from jax import lax
from jax.experimental import pallas as pl
from jax.experimental.pallas import tpu as pltpu
from jax.sharding import PartitionSpec as P

HEAD_SIZE = 64


def swapped(value, axis, apart):
    mask = 2**apart
    pairs = [(source, source ^ mask) for source in range(lax.axis_size(axis))]
    return lax.ppermute(value, axis, pairs)


def from_behind(block, axis, distance):
    devices = range(lax.axis_size(axis))
    route = [((i - distance) % len(devices), i) for i in devices]
    return lax.ppermute(block, axis, route)


def layer_norm(inputs, ln_gain, ln_bias):
    widened = inputs.astype(jnp.float32)
    average = jnp.mean(widened, -1, keepdims=True)
    centred = widened - average
    variance = jnp.mean(centred * centred, -1, keepdims=True)
    return (centred * lax.rsqrt(variance + 1e-05) * ln_gain + ln_bias).astype(jnp.bfloat16)


def attend(state_now, queries, key_part, value_part):
    running_max, running_sum, weighted = state_now
    key_count = key_part.shape[0]
    head_count = queries.shape[1]
    key_heads = key_part.reshape(key_count, head_count, HEAD_SIZE)
    value_heads = value_part.reshape(key_count, head_count, HEAD_SIZE)
    scores = jnp.einsum("qhd,khd->hqk", queries, key_heads, preferred_element_type=jnp.float32)
    new_max = jnp.maximum(running_max, jnp.max(scores, -1))
    rescale = jnp.exp(running_max - new_max)
    exponent = jnp.exp(scores - new_max[..., None])
    running_sum = running_sum * rescale + jnp.sum(exponent, -1)
    weights_bf = exponent.astype(jnp.bfloat16)
    weighted = weighted * rescale[..., None] + jnp.einsum(
        "hqk,khd->hqd", weights_bf, value_heads, preferred_element_type=jnp.float32
    )
    return (new_max, running_sum, weighted)


def empty_state(head_count, row_count):
    return (
        jnp.full((head_count, row_count), -jnp.inf, jnp.float32),
        jnp.zeros((head_count, row_count), jnp.float32),
        jnp.zeros((head_count, row_count, HEAD_SIZE), jnp.float32),
    )


def finish(final_state):
    mixed = final_state[2] / final_state[1][..., None]
    head_count, row_count = (mixed.shape[0], mixed.shape[1])
    return (
        jnp.transpose(mixed, (1, 0, 2))
        .reshape(row_count, head_count * HEAD_SIZE)
        .astype(jnp.bfloat16)
    )


def per_device_plain(inputs, ln_gain, ln_bias, qkv_weight, v_bias, out_weight, out_bias):
    normed = layer_norm(inputs, ln_gain, ln_bias)
    row_count = inputs.shape[0]
    head_width = v_bias.shape[0]
    head_count = head_width // HEAD_SIZE
    projected = jnp.dot(
        normed,
        lax.all_gather(qkv_weight, "tm", axis=0, tiled=True),
        preferred_element_type=jnp.float32,
    )
    queries = (projected[:, :head_width] * HEAD_SIZE ** (-0.5)).astype(jnp.bfloat16)
    key_rows = projected[:, head_width : 2 * head_width].astype(jnp.bfloat16)
    values = (projected[:, 2 * head_width :] + v_bias).astype(jnp.bfloat16)
    parity = lax.axis_index("tm") % 2
    half_count = head_count // 2
    half_width = half_count * HEAD_SIZE
    stacked = jnp.stack([queries, key_rows, values])
    keep_part = lax.dynamic_slice_in_dim(stacked, parity * half_width, half_width, 2)
    give_part = lax.dynamic_slice_in_dim(stacked, (1 - parity) * half_width, half_width, 2)
    got_part = swapped(give_part, "tm", 0)
    first_rows = jnp.where(parity == 0, keep_part, got_part)
    second_rows = jnp.where(parity == 0, got_part, keep_part)
    joined = jnp.concatenate([first_rows, second_rows], 1)
    pair_rows = 2 * row_count
    pair_queries = joined[0].reshape(pair_rows, half_count, HEAD_SIZE)
    key_value_block = joined[1:]
    state_now = attend(
        empty_state(half_count, pair_rows), pair_queries, key_value_block[0], key_value_block[1]
    )

    def cycle_turn(step, carry):
        state_now, block_now = carry
        block_now = from_behind(block_now, "tm", 2)
        return (attend(state_now, pair_queries, block_now[0], block_now[1]), block_now)

    final_state, unused_block = lax.fori_loop(
        0, lax.axis_size("tm") // 2 - 1, cycle_turn, (state_now, key_value_block)
    )
    pair_context = finish(final_state)
    mine_rows = lax.dynamic_slice_in_dim(pair_context, parity * row_count, row_count, 0)
    other_rows = lax.dynamic_slice_in_dim(pair_context, (1 - parity) * row_count, row_count, 0)
    back_rows = swapped(other_rows, "tm", 0)
    context = jnp.where(
        parity == 0,
        jnp.concatenate([mine_rows, back_rows], 1),
        jnp.concatenate([back_rows, mine_rows], 1),
    )
    projection = jnp.dot(
        context,
        lax.all_gather(out_weight, "tm", axis=1, tiled=True),
        preferred_element_type=jnp.float32,
    )
    return (inputs.astype(jnp.float32) + projection + out_bias).astype(jnp.bfloat16)


def fused_kernel(
    n,
    x_hbm, gain_hbm, bias_hbm, w_hbm, vb_hbm, wo_hbm, ob_hbm,
    o_ref,
    x_ref, gain_ref, bias_ref, w_ref, vb_ref, wo_ref, ob_ref, in_sem,
    xother, kv_bias, normed, wkv, wq, pass_kv, pass_q, kv, qh, top, total, acc, wofull, ctx, ctxfull,
    x_sem, wkv_send, wkv_recv, wq_send, wq_recv, kv_send, kv_recv, o_send, o_recv, c_sem,
):
    fetches = [
        pltpu.make_async_copy(source, target, in_sem.at[at])
        for at, (source, target) in enumerate(
            (
                (w_hbm, w_ref), (x_hbm, x_ref), (vb_hbm, vb_ref), (wo_hbm, wo_ref),
                (gain_hbm, gain_ref), (bias_hbm, bias_ref), (ob_hbm, ob_ref),
            )
        )
    ]
    for fetch in fetches:
        fetch.start()
    me = lax.axis_index("tm")
    lines = n // 4
    c = lax.rem(me, 2)
    y = lax.rem(lax.div(me, 2), 2)
    z = lax.div(me, 4)
    rows = x_ref.shape[0]
    wrows = w_ref.shape[0]
    width = wo_ref.shape[1]
    half = width // 2
    heads = half // HEAD_SIZE
    group = lax.axis_index("groups")
    side = lax.rem(group, 2)
    right, left = {"tm": me + 4}, {"tm": me - 4}
    has_right, has_left = z < lines - 1, z > 0
    other_y = {"tm": me + 2 - 4 * y}
    other_c = {"tm": me + 1 - 2 * c}
    other_x = {"groups": group + 1 - 2 * side}

    def send(src, dst, ssem, rsem, device):
        return pltpu.make_async_remote_copy(
            src_ref=src, dst_ref=dst, send_sem=ssem, recv_sem=rsem,
            device_id=device, device_id_type=pl.DeviceIdType.MESH,
        )

    def nth(t):
        near = jnp.minimum(z, lines - 1 - z)
        k = lax.div(t + 1, 2)
        both = jnp.where(lax.rem(t, 2) == 1, z - k, z + k)
        far = t - near
        one = jnp.where(z < lines - 1 - z, z + far, z - far)
        return jnp.where(t <= 2 * near, both, one)

    relayed = jnp.where(side == 0, y, 1 - y)

    def block_of(zz, yy, cc):
        return zz * 4 + yy * 2 + cc

    def block_rows(ref, block):
        return ref.at[pl.ds(pl.multiple_of(block * wrows, wrows), wrows), :]

    class Stream:
        def __init__(self, ref, ssem, rsem):
            self.ref, self.ssem, self.rsem = ref, ssem, rsem

        def copy(self, way, slot, zz, yy, cc, device, source=None):
            b = block_of(zz, yy, cc)
            there = block_rows(self.ref, b)
            return send(
                there if source is None else source, there, self.ssem.at[way, slot], self.rsem.at[b], device
            )

        def to_z(self, zz, yy):
            return self.copy(0, zz, z, yy, c, {"tm": block_of(zz, y, c)})

        def to_y(self, zz, source=None):
            return self.copy(1, zz, zz, y, c, other_y, source)

        def to_x(self, zz, yy):
            return self.copy(2, zz * 2 + yy, zz, yy, c, other_x)

        def to_c(self, zz, yy):
            return self.copy(3, zz * 2 + yy, zz, yy, c, other_c)

        def arrived(self, zz, yy, cc):
            self.copy(3, 0, zz, yy, cc, other_c).wait_recv()

    keys_values = Stream(wkv, wkv_send, wkv_recv)
    query_part = Stream(wq, wq_send, wq_recv)
    out_part = Stream(wofull, o_send, o_recv)

    def carried(zz):
        return lax.rem(zz + side, 2) == 0

    def each_other(act):
        def turn(t, carry):
            act(nth(t))
            return carry

        lax.fori_loop(1, lines, turn, 0)

    def each(act):
        def turn(zz, carry):
            act(zz)
            return carry

        lax.fori_loop(0, lines, turn, 0)

    def kv_z(zz, way, device):
        b = zz * 2 + c
        return send(kv.at[b], kv.at[b], kv_send.at[way, zz], kv_recv.at[b], device)

    def kv_c(zz, cc):
        b = zz * 2 + cc
        return send(kv.at[b], kv.at[b], kv_send.at[2, zz], kv_recv.at[b], other_c)

    def along(zz, makers):
        @pl.when(jnp.logical_and(zz <= z, has_right))
        def _():
            for maker in makers:
                maker(zz, 0, right).start()

        @pl.when(jnp.logical_and(zz >= z, has_left))
        def _():
            for maker in makers:
                maker(zz, 1, left).start()

    def along_done(zz, makers):
        @pl.when(jnp.logical_and(zz <= z, has_right))
        def _():
            for maker in makers:
                maker(zz, 0, right).wait_send()

        @pl.when(jnp.logical_and(zz >= z, has_left))
        def _():
            for maker in makers:
                maker(zz, 1, left).wait_send()

    barrier = pltpu.get_barrier_semaphore()

    def greet(device):
        pl.semaphore_signal(barrier, inc=1, device_id=device, device_id_type=pl.DeviceIdType.MESH)

    greet(other_y)
    greet(other_c)
    greet(other_x)
    each_other(lambda zz: greet({"tm": block_of(zz, y, c)}))

    kv_bias[...] = jnp.zeros_like(kv_bias)
    fetches[0].wait()
    fetches[2].wait()
    mine = pl.ds(pl.multiple_of(me * wrows, wrows), wrows)
    for yy in range(2):

        @pl.when(y == yy)
        def _():
            kv_bias[:, half:] = vb_ref[yy * half : (yy + 1) * half].reshape(1, half)
            for at, part in enumerate((1, 2)):
                wide = pl.ds(at * half, half)
                wkv[mine, wide] = w_ref[:, pl.ds(part * width + yy * half, half)]
                pass_kv[:, wide] = w_ref[:, pl.ds(part * width + (1 - yy) * half, half)]
            wq[mine, :half] = w_ref[:, pl.ds(yy * half, half)]
            pass_q[:, :half] = w_ref[:, pl.ds((1 - yy) * half, half)]

    pl.semaphore_wait(barrier, lines + 2)

    pairs = ((keys_values, pass_kv), (query_part, pass_q))

    def own_sends(stream):
        @pl.when(side == 0)
        def _():
            each_other(lambda zz: stream.to_z(zz, y).start())

        stream.to_c(z, y).start()

    def neighbour_sends(stream):
        stream.arrived(z, 1 - y, c)

        @pl.when(side == 1)
        def _():
            each_other(lambda zz: stream.to_z(zz, 1 - y).start())

        stream.to_c(z, 1 - y).start()

    keys_values.to_y(z, pass_kv).start()
    own_sends(keys_values)
    fetches[1].wait()
    x_copy = send(x_ref, xother, x_sem.at[0], x_sem.at[1], other_y)
    for fetch in fetches[3:]:
        fetch.wait()
    wofull[mine, :] = wo_ref[...]

    def norm_rows(ref, yy):
        widened = ref[...].astype(jnp.float32)
        average = jnp.mean(widened, -1, keepdims=True)
        centred = widened - average
        variance = jnp.mean(centred * centred, -1, keepdims=True)
        normed[pl.ds(pl.multiple_of(yy * rows, rows), rows), :] = (
            centred * lax.rsqrt(variance + 1e-05) * gain_ref[...] + bias_ref[...]
        ).astype(jnp.bfloat16)

    norm_rows(x_ref, y)

    neighbour_sends(keys_values)
    query_part.to_y(z, pass_q).start()
    x_copy.start()

    def spread_lines(stream):
        def act(zz):
            stream.arrived(zz, relayed, c)
            stream.to_x(zz, relayed).start()
            stream.to_c(zz, relayed).start()

        each_other(act)

    def spread_across(stream):
        def act(zz):
            stream.arrived(zz, 1 - relayed, c)
            stream.to_c(zz, 1 - relayed).start()

        each_other(act)

    def gathered(stream):
        def act(zz):
            for yy in range(2):
                stream.arrived(zz, yy, 1 - c)

        each(act)

    spread_lines(keys_values)
    own_sends(query_part)
    neighbour_sends(query_part)
    spread_across(keys_values)
    x_copy.wait()
    norm_rows(xother, 1 - y)
    gathered(keys_values)

    def out_first(zz):
        @pl.when(carried(zz))
        def _():
            out_part.arrived(zz, y, c)
            out_part.to_y(zz).start()
            out_part.to_x(zz, y).start()
            out_part.to_c(zz, y).start()

    def out_second(zz):
        @pl.when(carried(zz))
        def _():
            out_part.arrived(zz, 1 - y, c)
            out_part.to_x(zz, 1 - y).start()
            out_part.to_c(zz, 1 - y).start()

        @pl.when(jnp.logical_and(zz != z, jnp.logical_not(carried(zz))))
        def _():
            out_part.arrived(zz, y, c)
            out_part.to_c(zz, y).start()

    def out_third(zz):
        @pl.when(jnp.logical_not(carried(zz)))
        def _():
            out_part.arrived(zz, 1 - y, c)
            out_part.to_c(zz, 1 - y).start()

    own = z * 2 + c
    both = normed[...]
    kv[own] = (
        jnp.dot(both, wkv[...], preferred_element_type=jnp.float32) + kv_bias[...]
    ).astype(jnp.bfloat16)
    along(z, (kv_z,))
    kv_c(z, c).start()

    @pl.when(carried(z))
    def _():
        each_other(lambda zz: out_part.to_z(zz, y).start())
        out_part.to_y(z).start()

    out_part.to_c(z, y).start()
    spread_lines(query_part)
    spread_across(query_part)
    gathered(query_part)
    queries = (
        jnp.dot(both, wq[:, :half], preferred_element_type=jnp.float32) * HEAD_SIZE ** (-0.5)
    ).astype(jnp.bfloat16)
    for h in range(heads):
        qh[h] = queries[:, h * HEAD_SIZE : (h + 1) * HEAD_SIZE]
    top[...] = jnp.full_like(top, -jnp.inf)
    total[...] = jnp.zeros_like(total)
    acc[...] = jnp.zeros_like(acc)

    def attend_block(b):
        for h in range(heads):
            key_part = kv[b, :, h * HEAD_SIZE : (h + 1) * HEAD_SIZE]
            value_part = kv[b, :, half + h * HEAD_SIZE : half + (h + 1) * HEAD_SIZE]
            scores = lax.dot_general(
                qh[h], key_part, (((1,), (1,)), ((), ())), preferred_element_type=jnp.float32
            )
            old_top = top[h]
            new_top = jnp.maximum(old_top, jnp.max(scores, -1, keepdims=True))
            rescale = jnp.exp(old_top - new_top)
            exponent = jnp.exp(scores - new_top[:, :1])
            total[h] = total[h] * rescale + jnp.sum(exponent, -1, keepdims=True)
            top[h] = new_top
            acc[h] = acc[h] * rescale[:, :HEAD_SIZE] + jnp.dot(
                exponent.astype(jnp.bfloat16), value_part, preferred_element_type=jnp.float32
            )

    def kv_turn(t, carry):
        zz = nth(t)

        @pl.when(t > 0)
        def _():
            kv_z(zz, 0, right).wait_recv()
            along(zz, (kv_z,))
            kv_c(zz, c).start()

        attend_block(zz * 2 + c)
        kv_c(zz, 1 - c).wait_recv()
        attend_block(zz * 2 + 1 - c)

        @pl.when(t == min(1, lines - 1))
        def _():
            each_other(out_first)

        @pl.when(t == min(2, lines - 1))
        def _():
            each(out_second)

        @pl.when(t == min(3, lines - 1))
        def _():
            each(out_third)

        return carry

    lax.fori_loop(0, lines, kv_turn, 0)

    for h in range(heads):
        ctx[y, :, h * HEAD_SIZE : (h + 1) * HEAD_SIZE] = (
            acc[h] / total[h][:, :HEAD_SIZE]
        ).astype(jnp.bfloat16)
    theirs = pl.ds(pl.multiple_of((1 - y) * rows, rows), rows)
    ours = pl.ds(pl.multiple_of(y * rows, rows), rows)
    c_copy = send(ctx.at[y, theirs, :], ctx.at[y, theirs, :], c_sem.at[0], c_sem.at[1], other_y)
    c_back = send(ctx.at[1 - y, ours, :], ctx.at[1 - y, ours, :], c_sem.at[0], c_sem.at[1], other_y)
    c_copy.start()

    def drained(zz, carry):
        for stream, passed in pairs:
            for yy in range(2):
                stream.to_c(zz, yy).wait_send()

            @pl.when(zz != z)
            def _():
                stream.to_z(zz, relayed).wait_send()
                stream.to_x(zz, relayed).wait_send()

        for yy in range(2):
            out_part.to_c(zz, yy).wait_send()
            out_part.arrived(zz, yy, 1 - c)

        @pl.when(carried(zz))
        def _():
            out_part.to_y(zz).wait_send()
            out_part.to_x(zz, 1 - y).wait_send()

            @pl.when(zz != z)
            def _():
                out_part.to_x(zz, y).wait_send()

        @pl.when(jnp.logical_and(zz != z, carried(z)))
        def _():
            out_part.to_z(zz, y).wait_send()

        along_done(zz, (kv_z,))
        kv_c(zz, c).wait_send()
        return carry

    for stream, passed in pairs:
        stream.to_y(z, passed).wait_send()
    lax.fori_loop(0, lines, drained, 0)
    c_copy.wait_send()
    c_back.wait_recv()
    for part in range(2):
        ctxfull[:, part * half : (part + 1) * half] = ctx[part, ours, :half]
    projection = lax.dot_general(
        ctxfull[...], wofull[...], (((1,), (1,)), ((), ())), preferred_element_type=jnp.float32
    )
    o_ref[...] = (x_ref[...].astype(jnp.float32) + projection + ob_ref[...]).astype(o_ref.dtype)


def per_device_fused(n, inputs, ln_gain, ln_bias, qkv_weight, v_bias, out_weight, out_bias):
    rows, depth = inputs.shape
    width = v_bias.shape[0]
    half = width // 2
    heads = half // HEAD_SIZE
    lines = n // 4
    wrows = qkv_weight.shape[0]
    wide = pl.cdiv(half, 128) * 128
    dma = pltpu.SemaphoreType.DMA
    return pl.pallas_call(
        functools.partial(fused_kernel, n),
        out_shape=jax.ShapeDtypeStruct((rows, depth), jnp.bfloat16),
        in_specs=[pl.BlockSpec(memory_space=pltpu.HBM)] * 7,
        out_specs=pl.BlockSpec(memory_space=pltpu.VMEM),
        scratch_shapes=[
            pltpu.VMEM((rows, depth), jnp.bfloat16),
            pltpu.VMEM((depth,), jnp.float32),
            pltpu.VMEM((depth,), jnp.float32),
            pltpu.VMEM(qkv_weight.shape, jnp.bfloat16),
            pltpu.VMEM((width,), jnp.float32),
            pltpu.VMEM((wrows, width), jnp.bfloat16),
            pltpu.VMEM((depth,), jnp.float32),
            dma((7,)),
            pltpu.VMEM((rows, depth), jnp.bfloat16),
            pltpu.VMEM((1, 2 * half), jnp.float32),
            pltpu.VMEM((2 * rows, depth), jnp.bfloat16),
            pltpu.VMEM((depth, 2 * half), jnp.bfloat16),
            pltpu.VMEM((depth, wide), jnp.bfloat16),
            pltpu.VMEM((wrows, 2 * half), jnp.bfloat16),
            pltpu.VMEM((wrows, wide), jnp.bfloat16),
            pltpu.VMEM((2 * lines, 2 * rows, 2 * half), jnp.bfloat16),
            pltpu.VMEM((heads, 2 * rows, HEAD_SIZE), jnp.bfloat16),
            pltpu.VMEM((heads, 2 * rows, 128), jnp.float32),
            pltpu.VMEM((heads, 2 * rows, 128), jnp.float32),
            pltpu.VMEM((heads, 2 * rows, HEAD_SIZE), jnp.float32),
            pltpu.VMEM((depth, width), jnp.bfloat16),
            pltpu.VMEM((2, 2 * rows, wide), jnp.bfloat16),
            pltpu.VMEM((rows, width), jnp.bfloat16),
            dma((2,)),
            dma((4, 2 * lines)),
            dma((n,)),
            dma((4, 2 * lines)),
            dma((n,)),
            dma((3, lines)),
            dma((2 * lines,)),
            dma((4, 2 * lines)),
            dma((n,)),
            dma((2,)),
        ],
        compiler_params=pltpu.CompilerParams(
            collective_id=0, has_side_effects=True, vmem_limit_bytes=62 * 2**20
        ),
    )(inputs, ln_gain, ln_bias, qkv_weight, v_bias, out_weight.T, out_bias)


def per_device(inputs, ln_gain, ln_bias, qkv_weight, v_bias, out_weight, out_bias):
    n = lax.axis_size("tm")
    whole_tiles = (
        n % 4 == 0
        and lax.axis_size("groups") % 2 == 0
        and qkv_weight.shape[0] % 16 == 0
        and out_weight.shape[1] == qkv_weight.shape[0]
        and inputs.shape[0] % 16 == 0
        and v_bias.shape[0] % (2 * HEAD_SIZE) == 0
    )
    arguments = (inputs, ln_gain, ln_bias, qkv_weight, v_bias, out_weight, out_bias)
    if whole_tiles:
        return per_device_fused(n, *arguments)
    return per_device_plain(*arguments)


def solution(mesh):
    return jax.shard_map(
        per_device,
        mesh=mesh,
        in_specs=(P(("groups", "tm"), None), P(), P(), P("tm", None), P(), P(None, "tm"), P()),
        out_specs=P(("groups", "tm"), None),
        check_vma=False,
    )
```

```python
import functools

import jax
import jax.numpy as jnp
from jax import lax
from jax.experimental import pallas as pl
from jax.experimental.pallas import tpu as pltpu
from jax.sharding import PartitionSpec as P

HEAD_SIZE = 64


def swapped(value, axis, apart):
    mask = 2**apart
    pairs = [(source, source ^ mask) for source in range(lax.axis_size(axis))]
    return lax.ppermute(value, axis, pairs)


def from_behind(block, axis, distance):
    devices = range(lax.axis_size(axis))
    route = [((i - distance) % len(devices), i) for i in devices]
    return lax.ppermute(block, axis, route)


def layer_norm(inputs, ln_gain, ln_bias):
    widened = inputs.astype(jnp.float32)
    average = jnp.mean(widened, -1, keepdims=True)
    centred = widened - average
    variance = jnp.mean(centred * centred, -1, keepdims=True)
    return (centred * lax.rsqrt(variance + 1e-05) * ln_gain + ln_bias).astype(jnp.bfloat16)


def attend(state_now, queries, key_part, value_part):
    running_max, running_sum, weighted = state_now
    key_count = key_part.shape[0]
    head_count = queries.shape[1]
    key_heads = key_part.reshape(key_count, head_count, HEAD_SIZE)
    value_heads = value_part.reshape(key_count, head_count, HEAD_SIZE)
    scores = jnp.einsum("qhd,khd->hqk", queries, key_heads, preferred_element_type=jnp.float32)
    new_max = jnp.maximum(running_max, jnp.max(scores, -1))
    rescale = jnp.exp(running_max - new_max)
    exponent = jnp.exp(scores - new_max[..., None])
    running_sum = running_sum * rescale + jnp.sum(exponent, -1)
    weights_bf = exponent.astype(jnp.bfloat16)
    weighted = weighted * rescale[..., None] + jnp.einsum(
        "hqk,khd->hqd", weights_bf, value_heads, preferred_element_type=jnp.float32
    )
    return (new_max, running_sum, weighted)


def empty_state(head_count, row_count):
    return (
        jnp.full((head_count, row_count), -jnp.inf, jnp.float32),
        jnp.zeros((head_count, row_count), jnp.float32),
        jnp.zeros((head_count, row_count, HEAD_SIZE), jnp.float32),
    )


def finish(final_state):
    mixed = final_state[2] / final_state[1][..., None]
    head_count, row_count = (mixed.shape[0], mixed.shape[1])
    return (
        jnp.transpose(mixed, (1, 0, 2))
        .reshape(row_count, head_count * HEAD_SIZE)
        .astype(jnp.bfloat16)
    )


def per_device_plain(inputs, ln_gain, ln_bias, qkv_weight, v_bias, out_weight, out_bias):
    normed = layer_norm(inputs, ln_gain, ln_bias)
    row_count = inputs.shape[0]
    head_width = v_bias.shape[0]
    head_count = head_width // HEAD_SIZE
    projected = jnp.dot(
        normed,
        lax.all_gather(qkv_weight, "tm", axis=0, tiled=True),
        preferred_element_type=jnp.float32,
    )
    queries = (projected[:, :head_width] * HEAD_SIZE ** (-0.5)).astype(jnp.bfloat16)
    key_rows = projected[:, head_width : 2 * head_width].astype(jnp.bfloat16)
    values = (projected[:, 2 * head_width :] + v_bias).astype(jnp.bfloat16)
    parity = lax.axis_index("tm") % 2
    half_count = head_count // 2
    half_width = half_count * HEAD_SIZE
    stacked = jnp.stack([queries, key_rows, values])
    keep_part = lax.dynamic_slice_in_dim(stacked, parity * half_width, half_width, 2)
    give_part = lax.dynamic_slice_in_dim(stacked, (1 - parity) * half_width, half_width, 2)
    got_part = swapped(give_part, "tm", 0)
    first_rows = jnp.where(parity == 0, keep_part, got_part)
    second_rows = jnp.where(parity == 0, got_part, keep_part)
    joined = jnp.concatenate([first_rows, second_rows], 1)
    pair_rows = 2 * row_count
    pair_queries = joined[0].reshape(pair_rows, half_count, HEAD_SIZE)
    key_value_block = joined[1:]
    state_now = attend(
        empty_state(half_count, pair_rows), pair_queries, key_value_block[0], key_value_block[1]
    )

    def cycle_turn(step, carry):
        state_now, block_now = carry
        block_now = from_behind(block_now, "tm", 2)
        return (attend(state_now, pair_queries, block_now[0], block_now[1]), block_now)

    final_state, unused_block = lax.fori_loop(
        0, lax.axis_size("tm") // 2 - 1, cycle_turn, (state_now, key_value_block)
    )
    pair_context = finish(final_state)
    mine_rows = lax.dynamic_slice_in_dim(pair_context, parity * row_count, row_count, 0)
    other_rows = lax.dynamic_slice_in_dim(pair_context, (1 - parity) * row_count, row_count, 0)
    back_rows = swapped(other_rows, "tm", 0)
    context = jnp.where(
        parity == 0,
        jnp.concatenate([mine_rows, back_rows], 1),
        jnp.concatenate([back_rows, mine_rows], 1),
    )
    projection = jnp.dot(
        context,
        lax.all_gather(out_weight, "tm", axis=1, tiled=True),
        preferred_element_type=jnp.float32,
    )
    return (inputs.astype(jnp.float32) + projection + out_bias).astype(jnp.bfloat16)


def fused_kernel(
    n,
    x_hbm, gain_hbm, bias_hbm, w_hbm, vb_hbm, wo_hbm, ob_hbm,
    o_ref,
    x_ref, gain_ref, bias_ref, w_ref, vb_ref, wo_ref, ob_ref, in_sem,
    xother, kv_bias, normed, wkv, wq, pass_kv, pass_q, kv, qh, top, total, acc, wofull, ctx, ctxfull,
    x_sem, wkv_send, wkv_recv, wq_send, wq_recv, kv_send, kv_recv, o_send, o_recv, c_sem,
):
    fetches = [
        pltpu.make_async_copy(source, target, in_sem.at[at])
        for at, (source, target) in enumerate(
            (
                (w_hbm, w_ref), (x_hbm, x_ref), (vb_hbm, vb_ref), (wo_hbm, wo_ref),
                (gain_hbm, gain_ref), (bias_hbm, bias_ref), (ob_hbm, ob_ref),
            )
        )
    ]
    for fetch in fetches:
        fetch.start()
    me = lax.axis_index("tm")
    lines = n // 4
    c = lax.rem(me, 2)
    y = lax.rem(lax.div(me, 2), 2)
    z = lax.div(me, 4)
    rows = x_ref.shape[0]
    wrows = w_ref.shape[0]
    width = wo_ref.shape[1]
    half = width // 2
    heads = half // HEAD_SIZE
    group = lax.axis_index("groups")
    side = lax.rem(group, 2)
    right, left = {"tm": me + 4}, {"tm": me - 4}
    has_right, has_left = z < lines - 1, z > 0
    other_y = {"tm": me + 2 - 4 * y}
    other_c = {"tm": me + 1 - 2 * c}
    other_x = {"groups": group + 1 - 2 * side}

    def send(src, dst, ssem, rsem, device):
        return pltpu.make_async_remote_copy(
            src_ref=src, dst_ref=dst, send_sem=ssem, recv_sem=rsem,
            device_id=device, device_id_type=pl.DeviceIdType.MESH,
        )

    def nth(t):
        near = jnp.minimum(z, lines - 1 - z)
        k = lax.div(t + 1, 2)
        both = jnp.where(lax.rem(t, 2) == 1, z - k, z + k)
        far = t - near
        one = jnp.where(z < lines - 1 - z, z + far, z - far)
        return jnp.where(t <= 2 * near, both, one)

    relayed = jnp.where(side == 0, y, 1 - y)

    def block_of(zz, yy, cc):
        return zz * 4 + yy * 2 + cc

    def block_rows(ref, block):
        return ref.at[pl.ds(pl.multiple_of(block * wrows, wrows), wrows), :]

    class Stream:
        def __init__(self, ref, ssem, rsem):
            self.ref, self.ssem, self.rsem = ref, ssem, rsem

        def copy(self, way, slot, zz, yy, cc, device, source=None):
            b = block_of(zz, yy, cc)
            there = block_rows(self.ref, b)
            return send(
                there if source is None else source, there, self.ssem.at[way, slot], self.rsem.at[b], device
            )

        def to_z(self, zz, yy):
            return self.copy(0, zz, z, yy, c, {"tm": block_of(zz, y, c)})

        def to_y(self, zz, source=None):
            return self.copy(1, zz, zz, y, c, other_y, source)

        def to_x(self, zz, yy):
            return self.copy(2, zz * 2 + yy, zz, yy, c, other_x)

        def to_c(self, zz, yy):
            return self.copy(3, zz * 2 + yy, zz, yy, c, other_c)

        def arrived(self, zz, yy, cc):
            self.copy(3, 0, zz, yy, cc, other_c).wait_recv()

    keys_values = Stream(wkv, wkv_send, wkv_recv)
    query_part = Stream(wq, wq_send, wq_recv)
    out_part = Stream(wofull, o_send, o_recv)

    def carried(zz):
        return lax.rem(zz + side, 2) == 0

    def each_other(act):
        def turn(t, carry):
            act(nth(t))
            return carry

        lax.fori_loop(1, lines, turn, 0)

    def each(act):
        def turn(zz, carry):
            act(zz)
            return carry

        lax.fori_loop(0, lines, turn, 0)

    def kv_part(part, zz, way, device):
        b = zz * 2 + c
        there = kv.at[b, pl.ds(part * rows, rows), :]
        return send(there, there, kv_send.at[3 * part + way, zz], kv_recv.at[2 * lines * part + b], device)

    kv_parts = (functools.partial(kv_part, 0), functools.partial(kv_part, 1))

    def kv_c(zz, cc):
        b = zz * 2 + cc
        return send(kv.at[b], kv.at[b], kv_send.at[2, zz], kv_recv.at[b], other_c)

    def along(zz, makers):
        @pl.when(jnp.logical_and(zz <= z, has_right))
        def _():
            for maker in makers:
                maker(zz, 0, right).start()

        @pl.when(jnp.logical_and(zz >= z, has_left))
        def _():
            for maker in makers:
                maker(zz, 1, left).start()

    def along_done(zz, makers):
        @pl.when(jnp.logical_and(zz <= z, has_right))
        def _():
            for maker in makers:
                maker(zz, 0, right).wait_send()

        @pl.when(jnp.logical_and(zz >= z, has_left))
        def _():
            for maker in makers:
                maker(zz, 1, left).wait_send()

    barrier = pltpu.get_barrier_semaphore()

    def greet(device):
        pl.semaphore_signal(barrier, inc=1, device_id=device, device_id_type=pl.DeviceIdType.MESH)

    greet(other_y)
    greet(other_c)
    greet(other_x)
    each_other(lambda zz: greet({"tm": block_of(zz, y, c)}))

    kv_bias[...] = jnp.zeros_like(kv_bias)
    fetches[0].wait()
    fetches[2].wait()
    mine = pl.ds(pl.multiple_of(me * wrows, wrows), wrows)
    for yy in range(2):

        @pl.when(y == yy)
        def _():
            kv_bias[:, half:] = vb_ref[yy * half : (yy + 1) * half].reshape(1, half)
            for at, part in enumerate((1, 2)):
                wide = pl.ds(at * half, half)
                wkv[mine, wide] = w_ref[:, pl.ds(part * width + yy * half, half)]
                pass_kv[:, wide] = w_ref[:, pl.ds(part * width + (1 - yy) * half, half)]
            wq[mine, :half] = w_ref[:, pl.ds(yy * half, half)]
            pass_q[:, :half] = w_ref[:, pl.ds((1 - yy) * half, half)]

    pl.semaphore_wait(barrier, lines + 2)

    pairs = ((keys_values, pass_kv), (query_part, pass_q))

    def own_sends(stream):
        @pl.when(side == 0)
        def _():
            each_other(lambda zz: stream.to_z(zz, y).start())

        stream.to_c(z, y).start()

    def neighbour_sends(stream):
        stream.arrived(z, 1 - y, c)

        @pl.when(side == 1)
        def _():
            each_other(lambda zz: stream.to_z(zz, 1 - y).start())

        stream.to_c(z, 1 - y).start()

    keys_values.to_y(z, pass_kv).start()
    own_sends(keys_values)
    fetches[1].wait()
    x_copy = send(x_ref, xother, x_sem.at[0], x_sem.at[1], other_y)
    for fetch in fetches[3:]:
        fetch.wait()
    wofull[mine, :] = wo_ref[...]

    def norm_rows(ref, yy):
        widened = ref[...].astype(jnp.float32)
        average = jnp.mean(widened, -1, keepdims=True)
        centred = widened - average
        variance = jnp.mean(centred * centred, -1, keepdims=True)
        normed[pl.ds(pl.multiple_of(yy * rows, rows), rows), :] = (
            centred * lax.rsqrt(variance + 1e-05) * gain_ref[...] + bias_ref[...]
        ).astype(jnp.bfloat16)

    norm_rows(x_ref, y)

    neighbour_sends(keys_values)
    query_part.to_y(z, pass_q).start()
    x_copy.start()

    def spread_lines(stream):
        def act(zz):
            stream.arrived(zz, relayed, c)
            stream.to_x(zz, relayed).start()
            stream.to_c(zz, relayed).start()

        each_other(act)

    def spread_across(stream):
        def act(zz):
            stream.arrived(zz, 1 - relayed, c)
            stream.to_c(zz, 1 - relayed).start()

        each_other(act)

    def gathered(stream):
        def act(zz):
            for yy in range(2):
                stream.arrived(zz, yy, 1 - c)

        each(act)

    spread_lines(keys_values)
    own_sends(query_part)
    neighbour_sends(query_part)
    spread_across(keys_values)
    x_copy.wait()
    norm_rows(xother, 1 - y)
    gathered(keys_values)

    def out_first(zz):
        @pl.when(carried(zz))
        def _():
            out_part.arrived(zz, y, c)
            out_part.to_y(zz).start()
            out_part.to_x(zz, y).start()
            out_part.to_c(zz, y).start()

    def out_second(zz):
        @pl.when(carried(zz))
        def _():
            out_part.arrived(zz, 1 - y, c)
            out_part.to_x(zz, 1 - y).start()
            out_part.to_c(zz, 1 - y).start()

        @pl.when(jnp.logical_and(zz != z, jnp.logical_not(carried(zz))))
        def _():
            out_part.arrived(zz, y, c)
            out_part.to_c(zz, y).start()

    def out_third(zz):
        @pl.when(jnp.logical_not(carried(zz)))
        def _():
            out_part.arrived(zz, 1 - y, c)
            out_part.to_c(zz, 1 - y).start()

    own = z * 2 + c
    both = normed[...]
    kv[own] = (
        jnp.dot(both, wkv[...], preferred_element_type=jnp.float32) + kv_bias[...]
    ).astype(jnp.bfloat16)
    along(z, kv_parts)
    kv_c(z, c).start()

    @pl.when(carried(z))
    def _():
        each_other(lambda zz: out_part.to_z(zz, y).start())
        out_part.to_y(z).start()

    out_part.to_c(z, y).start()
    spread_lines(query_part)
    spread_across(query_part)
    gathered(query_part)
    queries = (
        jnp.dot(both, wq[:, :half], preferred_element_type=jnp.float32) * HEAD_SIZE ** (-0.5)
    ).astype(jnp.bfloat16)
    for h in range(heads):
        qh[h] = queries[:, h * HEAD_SIZE : (h + 1) * HEAD_SIZE]
    top[...] = jnp.full_like(top, -jnp.inf)
    total[...] = jnp.zeros_like(total)
    acc[...] = jnp.zeros_like(acc)

    def attend_block(b):
        for h in range(heads):
            key_part = kv[b, :, h * HEAD_SIZE : (h + 1) * HEAD_SIZE]
            value_part = kv[b, :, half + h * HEAD_SIZE : half + (h + 1) * HEAD_SIZE]
            scores = lax.dot_general(
                qh[h], key_part, (((1,), (1,)), ((), ())), preferred_element_type=jnp.float32
            )
            old_top = top[h]
            new_top = jnp.maximum(old_top, jnp.max(scores, -1, keepdims=True))
            rescale = jnp.exp(old_top - new_top)
            exponent = jnp.exp(scores - new_top[:, :1])
            total[h] = total[h] * rescale + jnp.sum(exponent, -1, keepdims=True)
            top[h] = new_top
            acc[h] = acc[h] * rescale[:, :HEAD_SIZE] + jnp.dot(
                exponent.astype(jnp.bfloat16), value_part, preferred_element_type=jnp.float32
            )

    def kv_turn(t, carry):
        zz = nth(t)

        @pl.when(t > 0)
        def _():
            for maker in kv_parts:
                maker(zz, 0, right).wait_recv()
                along(zz, (maker,))
            kv_c(zz, c).start()

        attend_block(zz * 2 + c)
        kv_c(zz, 1 - c).wait_recv()
        attend_block(zz * 2 + 1 - c)

        @pl.when(t == min(1, lines - 1))
        def _():
            each_other(out_first)

        @pl.when(t == min(2, lines - 1))
        def _():
            each(out_second)

        @pl.when(t == min(3, lines - 1))
        def _():
            each(out_third)

        return carry

    lax.fori_loop(0, lines, kv_turn, 0)

    for h in range(heads):
        ctx[y, :, h * HEAD_SIZE : (h + 1) * HEAD_SIZE] = (
            acc[h] / total[h][:, :HEAD_SIZE]
        ).astype(jnp.bfloat16)
    theirs = pl.ds(pl.multiple_of((1 - y) * rows, rows), rows)
    ours = pl.ds(pl.multiple_of(y * rows, rows), rows)
    c_copy = send(ctx.at[y, theirs, :], ctx.at[y, theirs, :], c_sem.at[0], c_sem.at[1], other_y)
    c_back = send(ctx.at[1 - y, ours, :], ctx.at[1 - y, ours, :], c_sem.at[0], c_sem.at[1], other_y)
    c_copy.start()

    def drained(zz, carry):
        for stream, passed in pairs:
            for yy in range(2):
                stream.to_c(zz, yy).wait_send()

            @pl.when(zz != z)
            def _():
                stream.to_z(zz, relayed).wait_send()
                stream.to_x(zz, relayed).wait_send()

        for yy in range(2):
            out_part.to_c(zz, yy).wait_send()
            out_part.arrived(zz, yy, 1 - c)

        @pl.when(carried(zz))
        def _():
            out_part.to_y(zz).wait_send()
            out_part.to_x(zz, 1 - y).wait_send()

            @pl.when(zz != z)
            def _():
                out_part.to_x(zz, y).wait_send()

        @pl.when(jnp.logical_and(zz != z, carried(z)))
        def _():
            out_part.to_z(zz, y).wait_send()

        along_done(zz, kv_parts)
        kv_c(zz, c).wait_send()
        return carry

    for stream, passed in pairs:
        stream.to_y(z, passed).wait_send()
    lax.fori_loop(0, lines, drained, 0)
    c_copy.wait_send()
    c_back.wait_recv()
    for part in range(2):
        ctxfull[:, part * half : (part + 1) * half] = ctx[part, ours, :half]
    projection = lax.dot_general(
        ctxfull[...], wofull[...], (((1,), (1,)), ((), ())), preferred_element_type=jnp.float32
    )
    o_ref[...] = (x_ref[...].astype(jnp.float32) + projection + ob_ref[...]).astype(o_ref.dtype)


def per_device_fused(n, inputs, ln_gain, ln_bias, qkv_weight, v_bias, out_weight, out_bias):
    rows, depth = inputs.shape
    width = v_bias.shape[0]
    half = width // 2
    heads = half // HEAD_SIZE
    lines = n // 4
    wrows = qkv_weight.shape[0]
    wide = pl.cdiv(half, 128) * 128
    dma = pltpu.SemaphoreType.DMA
    return pl.pallas_call(
        functools.partial(fused_kernel, n),
        out_shape=jax.ShapeDtypeStruct((rows, depth), jnp.bfloat16),
        in_specs=[pl.BlockSpec(memory_space=pltpu.HBM)] * 7,
        out_specs=pl.BlockSpec(memory_space=pltpu.VMEM),
        scratch_shapes=[
            pltpu.VMEM((rows, depth), jnp.bfloat16),
            pltpu.VMEM((depth,), jnp.float32),
            pltpu.VMEM((depth,), jnp.float32),
            pltpu.VMEM(qkv_weight.shape, jnp.bfloat16),
            pltpu.VMEM((width,), jnp.float32),
            pltpu.VMEM((wrows, width), jnp.bfloat16),
            pltpu.VMEM((depth,), jnp.float32),
            dma((7,)),
            pltpu.VMEM((rows, depth), jnp.bfloat16),
            pltpu.VMEM((1, 2 * half), jnp.float32),
            pltpu.VMEM((2 * rows, depth), jnp.bfloat16),
            pltpu.VMEM((depth, 2 * half), jnp.bfloat16),
            pltpu.VMEM((depth, wide), jnp.bfloat16),
            pltpu.VMEM((wrows, 2 * half), jnp.bfloat16),
            pltpu.VMEM((wrows, wide), jnp.bfloat16),
            pltpu.VMEM((2 * lines, 2 * rows, 2 * half), jnp.bfloat16),
            pltpu.VMEM((heads, 2 * rows, HEAD_SIZE), jnp.bfloat16),
            pltpu.VMEM((heads, 2 * rows, 128), jnp.float32),
            pltpu.VMEM((heads, 2 * rows, 128), jnp.float32),
            pltpu.VMEM((heads, 2 * rows, HEAD_SIZE), jnp.float32),
            pltpu.VMEM((depth, width), jnp.bfloat16),
            pltpu.VMEM((2, 2 * rows, wide), jnp.bfloat16),
            pltpu.VMEM((rows, width), jnp.bfloat16),
            dma((2,)),
            dma((4, 2 * lines)),
            dma((n,)),
            dma((4, 2 * lines)),
            dma((n,)),
            dma((6, lines)),
            dma((4 * lines,)),
            dma((4, 2 * lines)),
            dma((n,)),
            dma((2,)),
        ],
        compiler_params=pltpu.CompilerParams(
            collective_id=0, has_side_effects=True, vmem_limit_bytes=62 * 2**20
        ),
    )(inputs, ln_gain, ln_bias, qkv_weight, v_bias, out_weight.T, out_bias)


def per_device(inputs, ln_gain, ln_bias, qkv_weight, v_bias, out_weight, out_bias):
    n = lax.axis_size("tm")
    whole_tiles = (
        n % 4 == 0
        and lax.axis_size("groups") % 2 == 0
        and qkv_weight.shape[0] % 16 == 0
        and out_weight.shape[1] == qkv_weight.shape[0]
        and inputs.shape[0] % 16 == 0
        and v_bias.shape[0] % (2 * HEAD_SIZE) == 0
    )
    arguments = (inputs, ln_gain, ln_bias, qkv_weight, v_bias, out_weight, out_bias)
    if whole_tiles:
        return per_device_fused(n, *arguments)
    return per_device_plain(*arguments)


def solution(mesh):
    return jax.shard_map(
        per_device,
        mesh=mesh,
        in_specs=(P(("groups", "tm"), None), P(), P(), P("tm", None), P(), P(None, "tm"), P()),
        out_specs=P(("groups", "tm"), None),
        check_vma=False,
    )
```
